128 devices in a mesh: gx: 16 (over y, z), gy: 8 (over x, core).
Axes of the slice: x: 4, y: 4, z: 4, core: 2. Of those that a mesh axis runs over, the one named last changes fastest.
Arguments:
- soil_field: float32 [128, 64, 4, 256], P('gx', 'gy'), may hold values from 0 to 3
- rhizosphere: float32 [32768, 4, 128], P(('gx', 'gy')), may hold values from 0 to 1
- conductance: float32 [32768, 4, 128], P(('gx', 'gy')), may hold values from 0.02 to 0.45
- uptake_rate: float32 [32768, 4], P(('gx', 'gy')), may hold values from 0.02 to 0.45
- segment_weight: float32 [32768, 256], P(('gx', 'gy')), may hold values from 0.1 to 1
- segment_target: int32 [32768, 1], P(('gx', 'gy')), may hold values from 0 to 127; in each aligned block of 256 rows (0 to 255, 256 to 511, ...) at most 3 rows name the same one
- segment_tile: int32 [32768], P(('gx', 'gy')), may hold values from 0 to 63
- segment_count: int32 [128], P(('gx', 'gy')), may hold values from 1 to 256, 19660 in all
Outputs:
- rhizosphere_next: float32 [32768, 4, 128], P(('gx', 'gy'))
- soil_sink: float32 [128, 64, 4, 256], P('gx', 'gy')
The draws below stay inside these ranges and needn't reach their ends.
Inputs may be any that keep to these rules, and one draw needn't show every extreme that they name: `segment_target`: among the segment slots of one device no device is named by more than 3 slots, and some device is named by exactly 3. `segment_count`: some device has all 256 slots live.
All inputs are finite; a program needn't handle non-finite values.
Results may differ from the reference program's by a relative error of at most 0.00005.
Values sent between devices are 32-bit elements; how exact they have to be, the bound alone decides.
A program may use at most 128 MiB of HBM per device.

```python
import math
import jax
import jax.numpy as jnp
import numpy as np
from jax import lax

NF = 4
NR = 128
BLK = 256
SUB = 32
SEG_DEV = 256
BX = 8
BY = 8
CAP = 3
SEGS = 32768
NBX = 128
NBY = 64
N_GY = 8
DEVICES = 128


def place_ends(entries, own_key, low, high):
    shape = entries.shape
    place = [jax.random.randint(jax.random.fold_in(own_key, axis), (), 0, shape[axis]) for axis in range(len(shape))]
    entries = entries.at[tuple(place)].set(low)
    longest = shape.index(max(shape))
    place[longest] = (place[longest] + 1) % shape[longest]
    return entries.at[tuple(place)].set(high)


def level_of(own_key, extent, pieces, smallest, high):
    gain = 1.0
    for axis_at, shards_of in pieces:
        heights = jax.random.uniform(jax.random.fold_in(jax.random.fold_in(own_key, 6), axis_at), (shards_of,), jnp.float32, smallest / len(pieces), high / len(pieces))
        gain = gain * jnp.repeat(jnp.exp(heights), extent[axis_at] // shards_of).reshape((-1,) + (1,) * (len(extent) - 1 - axis_at))
    return gain


def split_up(number_of, total, bound, skew):
    weights = [(1 << 20) // math.isqrt(grade ** skew) + 1 for grade in range(2, number_of + 1)]
    surplus, counts = total - bound - (number_of - 1), [1] * (number_of - 1)
    while surplus > 0:
        candidates = [i for i in range(number_of - 1) if counts[i] < bound]
        whole, left = sum([weights[i] for i in candidates]), surplus
        for i in candidates:
            more = min(bound - counts[i], max(1, left * weights[i] // whole), surplus)
            counts[i] = counts[i] + more
            surplus = surplus - more
    return np.array([bound] + counts)


def uneven_parts(key, number_of, total, most, skew):
    if number_of == 2:
        one = jax.random.randint(key, (), max(1, total - most), min(most, total - 1) + 1)
        return jnp.stack([one, total - one])
    sizes = jnp.asarray(split_up(number_of, total, most, skew), jnp.int32)
    twos = (number_of - 1) // 2
    source_of, taker = sizes[1:1 + 2 * twos:2], sizes[2:2 + 2 * twos:2]
    slack = jnp.minimum(source_of - 1, most - taker)
    passed = jax.random.randint(jax.random.fold_in(key, 1), (twos,), 0, 1 << 20) % (slack + 1)
    sizes = sizes.at[1:1 + 2 * twos:2].set(source_of - passed).at[2:2 + 2 * twos:2].set(taker + passed)
    return sizes[jax.random.permutation(jax.random.fold_in(key, 2), number_of)]


def shared_out(key, own, number, rows, count, top, limit, lean):
    sequence = jax.random.permutation(key, count)
    packed, ordinary = portions_of(count, rows * top, limit, lean, True), portions_of(count, rows * top, limit, lean, False)
    places = jnp.arange(count)

    def named(lengths, offset_by):
        used = int((lengths > 0).sum())
        fixed = max(1, used // 4)
        shifted = fixed + (places - fixed + offset_by * (used - fixed)) % max(1, count - fixed)
        return jnp.zeros((count,), jnp.int32).at[sequence[jnp.where(places < fixed, places, shifted)]].set(jnp.asarray(lengths, jnp.int32))

    lengths = jnp.where(number % 4 == 0, named(packed, number // 4), named(ordinary, number - number // 4 - 1))
    mixed = jax.random.permutation(jax.random.fold_in(own, 3), count)
    giver, taker = mixed[0:count // 2 * 2:2], mixed[1:count // 2 * 2:2]
    slack = jnp.minimum(lengths[giver] - 1, limit - lengths[taker]) // 2
    slack = jnp.where((giver == sequence[0]) | (taker == sequence[0]) | (lengths[taker] == 0), 0, jnp.maximum(slack, 0))
    shifted = jax.random.randint(jax.random.fold_in(own, 4), (count // 2,), 0, 1 << 20) % (slack + 1)
    lengths = lengths.at[giver].add(-shifted).at[taker].add(shifted)
    labels = jnp.searchsorted(jnp.cumsum(lengths), jnp.arange(rows * top), side="right").astype(jnp.int32)
    grid = labels.reshape(top, rows).T
    grid = grid[jax.random.permutation(jax.random.fold_in(own, 1), rows)]
    offset_by = jax.random.randint(jax.random.fold_in(own, 2), (rows, 1), 0, top)
    return jnp.take_along_axis(grid, (jnp.arange(top)[None, :] + offset_by) % top, axis=1)


def portions_of(amount, total, reach, lean, full):
    weights = [(1 << 20) // math.isqrt(standing ** lean) + 1 for standing in range(1, amount + 1)]
    largest = reach if full else min(reach, max(-(-total // amount), total * weights[0] // sum(weights)))
    least = 1 if total - largest >= amount - 1 else 0
    counts, rest = [largest] + [least] * (amount - 1), total - largest - least * (amount - 1)
    while rest > 0:
        candidates = [i for i in range(1, amount) if counts[i] < largest] or [i for i in range(1, amount) if counts[i] < reach]
        pool, left = sum([weights[i] for i in candidates]), rest
        for i in candidates:
            more = min(reach - counts[i], max(1, left * weights[i] // pool), rest)
            counts[i] = counts[i] + more
            rest = rest - more
    return np.array(counts)


def setup_inputs(seed: int = 0) -> dict:
    streams_of = jax.random.split(jax.random.key(seed), 9)
    soil_field = jnp.clip(3.0 * jax.random.uniform(streams_of[0], (NBX, NBY, NF, BLK), jnp.float32) ** level_of(streams_of[0], (NBX, NBY, NF, BLK), ((0, 16), (1, 8)), -0.2, 0.2), 0.0, 3.0)
    rhizosphere = jnp.clip(1.0 * jax.random.uniform(streams_of[1], (SEGS, NF, NR), jnp.float32) ** level_of(streams_of[1], (SEGS, NF, NR), ((0, 128),), -0.2, 0.2), 0.0, 1.0)
    conductance = jnp.clip(jnp.exp(math.log(0.45) - 3.1135153 * jax.random.uniform(streams_of[2], (SEGS, NF, NR), jnp.float32) ** level_of(streams_of[2], (SEGS, NF, NR), ((0, 128),), -0.2, 0.2)), 0.02, 0.45)
    uptake_rate = jnp.clip(jnp.exp(math.log(0.45) - 3.1135153 * jax.random.uniform(streams_of[3], (SEGS, NF), jnp.float32) ** level_of(streams_of[3], (SEGS, NF), ((0, 128),), -0.2, 0.2)), 0.02, 0.45)
    segment_weight = jnp.clip(jnp.exp(math.log(1.0) - 2.3025851 * jax.random.uniform(streams_of[4], (SEGS, BLK), jnp.float32) ** level_of(streams_of[4], (SEGS, BLK), ((0, 128),), -0.2, 0.2)), 0.1, 1.0)
    segment_target_keys = jax.random.split(jax.random.fold_in(streams_of[5], 1), SEGS // SEG_DEV)
    segment_target_turns = jax.random.permutation(jax.random.fold_in(streams_of[5], 3), SEGS // SEG_DEV)
    segment_target = jax.vmap(lambda own, number: shared_out(jax.random.fold_in(streams_of[5], 2), own, number, SEG_DEV, DEVICES, 1, CAP, 2))(segment_target_keys, segment_target_turns).reshape((SEGS, 1))
    segment_tile = place_ends(jax.random.randint(streams_of[6], (SEGS,), 0, BX * BY), jax.random.fold_in(streams_of[6], 1), 0, (BX * BY) - 1).astype(jnp.int32)
    segment_count = uneven_parts(streams_of[7], DEVICES, DEVICES * SEG_DEV * 3 // 5, SEG_DEV, 2).astype(jnp.int32)
    return dict(soil_field=soil_field, rhizosphere=rhizosphere, conductance=conductance, uptake_rate=uptake_rate, segment_weight=segment_weight, segment_target=segment_target, segment_tile=segment_tile, segment_count=segment_count)


def radial_steps(profile, conductance, uptake_rate, boundary):
    def substep(step, state_pair):
        level, drawn = state_pair
        outward = jnp.concatenate([level[:, :, 1:], boundary[:, :, None]], axis=2)
        current = conductance * (outward - level)
        absorbed = uptake_rate[:, :, None] * level[:, :, :1]
        incoming = jnp.concatenate([absorbed, current[:, :, :-1]], axis=2)
        return level + current - incoming, drawn + current[:, :, -1]
    start = (profile, jnp.zeros(profile.shape[:2], jnp.float32))
    return lax.fori_loop(0, SUB, substep, start)


def reference(soil_field, rhizosphere, conductance, uptake_rate, segment_weight, segment_target, segment_tile, segment_count):
    numbering = jnp.arange(SEGS, dtype=jnp.int32)
    holder = numbering // SEG_DEV
    active = (numbering % SEG_DEV) < segment_count[holder]
    target = segment_target[:, 0]
    tile_row = (target // N_GY) * BX + segment_tile // BY
    tile_col = (target % N_GY) * BY + segment_tile % BY
    gathered = soil_field[tile_row, tile_col]
    weight_total = jnp.sum(segment_weight, axis=1)
    boundary = jnp.einsum("sfv,sv->sf", gathered, segment_weight, precision=lax.Precision.HIGHEST) / weight_total[:, None]
    boundary = jnp.where(active[:, None], boundary, 0.0)
    profile, drawn = radial_steps(rhizosphere, conductance, uptake_rate, boundary)
    rhizosphere_next = jnp.where(active[:, None, None], profile, rhizosphere)
    drawn = jnp.where(active[:, None], drawn, 0.0)
    portion = segment_weight / weight_total[:, None]
    uptake_rows = drawn[:, :, None] * portion[:, None, :]
    collected = jax.ops.segment_sum(uptake_rows, tile_row * NBY + tile_col, num_segments=NBX * NBY)
    soil_sink = collected.reshape(NBX, NBY, NF, BLK)
    return rhizosphere_next, soil_sink
```

```python
import itertools

import jax
import jax.numpy as jnp
from jax import lax
from jax.experimental import pallas as pl
from jax.experimental.pallas import tpu as pltpu
from jax.sharding import PartitionSpec as P

SUB = 32
CAP = 3
NR = 128
F32 = jnp.float32
BF16 = jnp.bfloat16
MESH = pl.DeviceIdType.MESH
NN = (((1,), (0,)), ((), ()))
NT = (((1,), (1,)), ((), ()))


def hops(o):
    return sum(min(v, 4 - v) for v in o[:3])


OFFSETS = sorted(
    (o for o in itertools.product(range(4), range(4), range(4), range(2)) if any(o)),
    key=lambda o: (-hops(o), o),
)


def coords():
    gx, gy = lax.axis_index("gx"), lax.axis_index("gy")
    return gy // 2, gx // 4, lax.rem(gx, 4), lax.rem(gy, 2)


def partner(here, o):
    x, y, z, c = here
    gx = ((y + o[1]) & 3) * 4 + ((z + o[2]) & 3)
    gy = ((x + o[0]) & 3) * 2 + (c ^ o[3])
    return gx, gy


def dot(a, b, dims=NN):
    return lax.dot_general(a, b, dims, preferred_element_type=F32)


def split2(x):
    high = x.astype(BF16)
    return high, (x - high.astype(F32)).astype(BF16)


def split3(x):
    high, mid = split2(x)
    return high, mid, (x - high.astype(F32) - mid.astype(F32)).astype(BF16)


def row(r):
    return pl.ds(8 * r, 8)


def double_step(level, cond, low, boundary, uptake):
    l0 = level[row(low), :]
    zero = jnp.zeros((8, 128), F32)
    p0 = uptake * l0 if uptake is not None else zero
    p1 = l1 = cp = None
    for r in range(low, NR):
        c = cond[row(r), :]
        outer = level[row(r + 1), :] if r < NR - 1 else boundary
        cur = c * (outer - l0)
        new = l0 + cur - p0 if p0 is not None else l0 + cur
        p0, l0 = cur, outer
        if r == low:
            p1 = uptake * new if uptake is not None else zero
        else:
            cur1 = cp * (new - l1)
            level[row(r - 1), :] = l1 + cur1 - p1
            p1 = cur1
        l1, cp = new, c
    cur1 = cp * (boundary - l1)
    level[row(NR - 1), :] = l1 + cur1 - p1
    return p0 + cur1


def kernel(
    soil_h, rhiz_h, cond_h, upt_h, w_h, tgt_h, tile_h, cnt_s,
    next_o, sink_o,
    soil_v, rhiz_v, cond_v, upt_v, w_v, tgt_v, tile_v, next_v, sink_v,
    pm, cm, tm, um, sel, sb, rb, qb, ret,
    in_sems, out_sems, send_sem, recv_sem, send2_sem, recv2_sem,
):
    here = coords()
    me = lax.axis_index("gx") * 8 + lax.axis_index("gy")
    loads = [
        pltpu.make_async_copy(s, d, in_sems.at[i])
        for i, (s, d) in enumerate(
            [(tgt_h, tgt_v), (tile_h, tile_v), (w_h, w_v), (cond_h, cond_v), (rhiz_h, rhiz_v), (upt_h, upt_v), (soil_h, soil_v)]
        )
    ]
    for c in loads:
        c.start()
    barrier = pltpu.get_barrier_semaphore()
    for o in OFFSETS:
        pl.semaphore_signal(barrier, inc=1, device_id=partner(here, o), device_id_type=MESH)
    count = cnt_s[0]

    for c in loads[:3]:
        c.wait()
    live = lax.broadcasted_iota(jnp.int32, (1, 256), 1) < count
    names = lax.broadcasted_iota(jnp.int32, (128, 256), 0)
    match = jnp.where((names == tgt_v[...]) & live, 1.0, 0.0)
    before = jnp.where(
        lax.broadcasted_iota(jnp.int32, (256, 256), 0) < lax.broadcasted_iota(jnp.int32, (256, 256), 1), 1.0, 0.0
    ).astype(BF16)
    rank = dot(match.astype(BF16), before)
    for k in range(CAP):
        sel[pl.ds(128 * k, 128), :] = jnp.where(rank == k, match, 0.0).astype(BF16)
    w = w_v[...]
    portion = w / jnp.sum(w, axis=1, keepdims=True)
    high, mid = split2(portion)
    for k in range(CAP):
        pick = sel[pl.ds(128 * k, 128), :]
        rows = dot(pick, high) + dot(pick, mid)
        sb[pl.ds(2 * k, 128, stride=8), :] = rows[:, :128]
        sb[pl.ds(2 * k + 1, 128, stride=8), :] = rows[:, 128:]

    for c in loads[3:6]:
        c.wait()
    lives = [lax.broadcasted_iota(jnp.int32, (1, 128), 1) + 128 * half < count for half in range(2)]
    for j in range(8):
        half, f = j // 4, j % 4
        block = pl.ds(512 * half + f, 128, stride=4)
        pm[pl.ds(j, 128, stride=8), :] = rhiz_v[block, :].T
        cm[pl.ds(j, 128, stride=8), :] = jnp.where(lives[half], cond_v[block, :].T, 0.0)
    uptake = jnp.concatenate(
        [jnp.where(lives[half], upt_v[:, pl.ds(128 * half, 128)], 0.0) for half in range(2)], axis=0
    )

    zero, one = jnp.zeros((8, 128), F32), jnp.ones((8, 128), F32)
    for r in range(NR - 32, NR):
        tm[row(r), :] = pm[row(r), :]
        um[row(r), :] = zero
    drawn0, gain = zero, zero
    for g in range(4):
        drawn0 = lax.fori_loop(0, 4, lambda i, d, g=g: d + double_step(tm, cm, NR - 32 + 8 * g, zero, None), drawn0)
        gain = lax.fori_loop(0, 4, lambda i, d, g=g: d + double_step(um, cm, NR - 8 - 8 * g, one, None), gain)

    def as_rows(v):
        return jnp.concatenate([v[0:4], v[4:8]], axis=1)

    tile_row = tile_v[...].astype(F32)
    items = jnp.concatenate(
        [tile_row, jnp.zeros((3, 256), F32), as_rows(drawn0), as_rows(gain), jnp.zeros((4, 256), F32)], axis=0
    )
    meta = jnp.zeros((128, 128), F32)
    for k in range(CAP):
        parts = [jnp.zeros((16 * k, 256), F32)] if k else []
        wide = jnp.concatenate(parts + [items, jnp.zeros((112 - 16 * k, 256), F32)], axis=0)
        pick = sel[pl.ds(128 * k, 128), :]
        for piece in split3(wide):
            meta = meta + dot(pick, piece, NT)
    sb[pl.ds(6, 128, stride=8), :] = meta
    sb[pl.ds(7, 128, stride=8), :] = jnp.zeros((128, 128), F32)

    pl.semaphore_wait(barrier, len(OFFSETS))
    for o in OFFSETS:
        gx, gy = partner(here, o)
        pltpu.make_async_remote_copy(
            sb.at[row(gx * 8 + gy), :], rb.at[row(me), :], send_sem, recv_sem, device_id=(gx, gy), device_id_type=MESH
        ).start()
    rb[row(me), :] = sb[row(me), :]

    lax.fori_loop(0, SUB // 2, lambda i, d: d + double_step(pm, cm, 0, zero, uptake), zero)
    loads[6].wait()
    soil = jnp.concatenate(
        [
            jnp.concatenate([soil_v[pl.ds(4 * half + f, 64, stride=8), :] for half in range(2)], axis=1)
            for f in range(4)
        ],
        axis=0,
    )
    soil_high, soil_mid = split2(soil)

    view = rb.at[pl.ds(0, 8 * 127), :]
    pltpu.make_async_copy(view, view, recv_sem).wait()
    got = jnp.concatenate(
        [
            jnp.concatenate([rb[pl.ds(2 * k + half, 128, stride=8), :] for half in range(2)], axis=1)
            for k in range(CAP)
        ],
        axis=0,
    )
    got_high, got_mid = split2(got)
    field = dot(soil_high, got_high, NT) + dot(soil_high, got_mid, NT) + dot(soil_mid, got_high, NT)
    info = rb[pl.ds(6, 128, stride=8), :].T
    tiles = (lax.broadcasted_iota(jnp.int32, (256, 128), 0) & 63).astype(F32)
    marks, values = [], []
    for k in range(CAP):
        mark = tiles == info[16 * k : 16 * k + 1]
        masked = jnp.where(mark, field[:, 128 * k : 128 * k + 128], 0.0)
        marks.append(mark)
        values.append([jnp.sum(masked[64 * f : 64 * f + 64], axis=0, keepdims=True) for f in range(4)])
    reply = jnp.concatenate(
        [jnp.concatenate(values[k] + [jnp.zeros((4, 128), F32)], axis=0) for k in range(CAP)]
        + [jnp.zeros((128 - 8 * CAP, 128), F32)],
        axis=0,
    )
    qb[:, 0, :] = reply.T
    for o in OFFSETS:
        gx, gy = partner(here, o)
        pltpu.make_async_remote_copy(
            qb.at[gx * 8 + gy], ret.at[me], send2_sem, recv2_sem, device_id=(gx, gy), device_id_type=MESH
        ).start()
    ret[me] = qb[me]

    share = []
    for k in range(CAP):
        drawn = [
            info[16 * k + 4 + f : 16 * k + 5 + f] + info[16 * k + 8 + f : 16 * k + 9 + f] * values[k][f]
            for f in range(4)
        ]
        spread = jnp.concatenate([jnp.broadcast_to(d, (64, 128)) for d in drawn], axis=0)
        share.append(jnp.where(marks[k], spread, 0.0))
    share_high, share_mid = split2(jnp.concatenate(share, axis=1))
    sink = dot(share_high, got_high) + dot(share_high, got_mid) + dot(share_mid, got_high)
    for f in range(4):
        for half in range(2):
            sink_v[pl.ds(4 * half + f, 64, stride=8), :] = sink[64 * f : 64 * f + 64, 128 * half : 128 * half + 128]
    sink_out = pltpu.make_async_copy(sink_v, sink_o, out_sems.at[0])
    sink_out.start()

    view = ret.at[pl.ds(0, 127)]
    pltpu.make_async_copy(view, view, recv2_sem).wait()
    back = ret[:, 0, :].T
    bound = jnp.zeros((8, 256), F32)
    for k in range(CAP):
        pick = sel[pl.ds(128 * k, 128), :]
        for piece in split3(back[8 * k : 8 * k + 8]):
            bound = bound + dot(piece, pick)
    bound = jnp.concatenate([bound[0:4, :128], bound[0:4, 128:]], axis=0)
    for r in range(NR - 32, NR):
        pm[row(r), :] = pm[row(r), :] + bound * um[row(r), :]
    for j in range(8):
        half, f = j // 4, j % 4
        next_v[pl.ds(512 * half + f, 128, stride=4), :] = pm[pl.ds(j, 128, stride=8), :].T
    next_out = pltpu.make_async_copy(next_v, next_o, out_sems.at[1])
    next_out.start()

    view = sb.at[pl.ds(0, 8 * 127), :]
    pltpu.make_async_copy(view, view, send_sem).wait()
    view = qb.at[pl.ds(0, 127)]
    pltpu.make_async_copy(view, view, send2_sem).wait()
    sink_out.wait()
    next_out.wait()


def on_device(
    soil_field, rhizosphere, conductance, uptake_rate, segment_weight, segment_target, segment_tile, segment_count
):
    soil = soil_field.reshape(64, 4, 2, 128).transpose(0, 2, 1, 3).reshape(512, 128)
    vm = pltpu.VMEM
    any_spec = pl.BlockSpec(memory_space=pl.ANY)
    nxt, sink = pl.pallas_call(
        kernel,
        out_shape=(jax.ShapeDtypeStruct((1024, 128), F32), jax.ShapeDtypeStruct((512, 128), F32)),
        in_specs=[any_spec] * 7 + [pl.BlockSpec(memory_space=pltpu.SMEM)],
        out_specs=(any_spec, any_spec),
        scratch_shapes=[
            vm((512, 128), F32), vm((1024, 128), F32), vm((1024, 128), F32), vm((4, 256), F32), vm((256, 256), F32),
            vm((1, 256), jnp.int32), vm((1, 256), jnp.int32), vm((1024, 128), F32), vm((512, 128), F32),
            vm((1024, 128), F32), vm((1024, 128), F32), vm((1024, 128), F32), vm((1024, 128), F32),
            vm((384, 256), BF16), vm((1024, 128), F32), vm((1024, 128), F32),
            vm((128, 1, 128), F32), vm((128, 1, 128), F32),
            pltpu.SemaphoreType.DMA((7,)), pltpu.SemaphoreType.DMA((2,)),
            pltpu.SemaphoreType.DMA(()), pltpu.SemaphoreType.DMA(()),
            pltpu.SemaphoreType.DMA(()), pltpu.SemaphoreType.DMA(()),
        ],
        compiler_params=pltpu.CompilerParams(
            collective_id=0, has_side_effects=True, vmem_limit_bytes=60 * 1024 * 1024
        ),
    )(
        soil,
        rhizosphere.reshape(1024, 128),
        conductance.reshape(1024, 128),
        uptake_rate.T,
        segment_weight,
        segment_target.reshape(1, 256),
        segment_tile.reshape(1, 256),
        segment_count,
    )
    sink = sink.reshape(64, 2, 4, 128).transpose(0, 2, 1, 3)
    return nxt.reshape(256, 4, 128), sink.reshape(8, 8, 4, 256)


def solution(mesh):
    flat = ("gx", "gy")
    return jax.shard_map(
        on_device,
        mesh=mesh,
        in_specs=(
            P("gx", "gy", None, None), P(flat, None, None), P(flat, None, None), P(flat, None), P(flat, None),
            P(flat, None), P(flat), P(flat),
        ),
        out_specs=(P(flat, None, None), P("gx", "gy", None, None)),
        check_vma=False,
    )
```

```python
import itertools

import jax
import jax.numpy as jnp
from jax import lax
from jax.experimental import pallas as pl
from jax.experimental.pallas import tpu as pltpu
from jax.sharding import PartitionSpec as P

SUB = 32
CAP = 3
NR = 128
F32 = jnp.float32
BF16 = jnp.bfloat16
MESH = pl.DeviceIdType.MESH
NN = (((1,), (0,)), ((), ()))
NT = (((1,), (1,)), ((), ()))


MESSAGE = 7


def hops(o):
    return sum(min(v, 4 - v) for v in o[:2])


PLANE = sorted((o for o in itertools.product(range(4), range(4), range(2)) if any(o)), key=lambda o: (-hops(o), o))


def coords():
    gx, gy = lax.axis_index("gx"), lax.axis_index("gy")
    return gy // 2, gx // 4, lax.rem(gx, 4), lax.rem(gy, 2)


def device(x, y, z, c):
    return y * 4 + z, x * 2 + c


def place(x, y, z, c):
    return z * 32 + y * 8 + x * 2 + c


def dot(a, b, dims=NN):
    return lax.dot_general(a, b, dims, preferred_element_type=F32)


def split2(x):
    high = x.astype(BF16)
    return high, (x - high.astype(F32)).astype(BF16)


def split3(x):
    high, mid = split2(x)
    return high, mid, (x - high.astype(F32) - mid.astype(F32)).astype(BF16)


def row(r):
    return pl.ds(8 * r, 8)


def double_step(level, cond, low, boundary, uptake):
    l0 = level[row(low), :]
    zero = jnp.zeros((8, 128), F32)
    p0 = uptake * l0 if uptake is not None else zero
    p1 = l1 = cp = None
    for r in range(low, NR):
        c = cond[row(r), :]
        outer = level[row(r + 1), :] if r < NR - 1 else boundary
        cur = c * (outer - l0)
        new = l0 + cur - p0 if p0 is not None else l0 + cur
        p0, l0 = cur, outer
        if r == low:
            p1 = uptake * new if uptake is not None else zero
        else:
            cur1 = cp * (new - l1)
            level[row(r - 1), :] = l1 + cur1 - p1
            p1 = cur1
        l1, cp = new, c
    cur1 = cp * (boundary - l1)
    level[row(NR - 1), :] = l1 + cur1 - p1
    return p0 + cur1


def exchange(
    soil_h, rhiz_h, cond_h, upt_h, w_h, tgt_h, tile_h, cnt_s,
    pm_o, um_o, sel_o, sink_o, ret,
    soil_v, rhiz_v, cond_v, upt_v, w_v, tgt_v, tile_v, sink_v,
    pm, cm, tm, um, sel, sb, rb, qb, info_v,
    in_sems, out_sems, plane_sem, send_sem, recv_sem, send2_sem, recv2_sem,
):
    x, y, z, c = coords()
    me = place(x, y, z, c)
    loads = [
        pltpu.make_async_copy(s, d, in_sems.at[i])
        for i, (s, d) in enumerate(
            [(tgt_h, tgt_v), (tile_h, tile_v), (w_h, w_v), (cond_h, cond_v), (rhiz_h, rhiz_v), (upt_h, upt_v), (soil_h, soil_v)]
        )
    ]
    for load in loads:
        load.start()

    def beside(o):
        return (x + o[0]) & 3, (y + o[1]) & 3, c ^ o[2]

    barrier = pltpu.get_barrier_semaphore()
    for dz in (2, 1, 3):
        pl.semaphore_signal(barrier, inc=1, device_id=device(x, y, (z + dz) & 3, c), device_id_type=MESH)
    for o in PLANE:
        ox, oy, oc = beside(o)
        pl.semaphore_signal(barrier, inc=1, device_id=device(ox, oy, z, oc), device_id_type=MESH)
    count = cnt_s[0]

    def send(p, src, dst, send_s, recv_s, rows):
        def copy_to(x, y, c):
            there = place(x, y, p, c)
            return pltpu.make_async_remote_copy(
                src.at[rows(there)], dst.at[rows(me)], send_s, recv_s.at[z],
                device_id=device(x, y, p, c), device_id_type=MESH,
            )

        for o in PLANE:
            copy_to(*beside(o)).start()

        @pl.when(z != p)
        def _():
            copy_to(x, y, c).start()

        @pl.when(z == p)
        def _():
            pltpu.make_async_copy(src.at[rows(me)], dst.at[rows(me)], recv_s.at[z]).start()

    def block(r):
        return pl.ds(8 * r, MESSAGE)

    for load in loads[:3]:
        load.wait()
    live = lax.broadcasted_iota(jnp.int32, (1, 256), 1) < count
    names = lax.broadcasted_iota(jnp.int32, (128, 256), 0)
    target = tgt_v[...]
    target = ((target >> 3) & 3) * 32 + (target >> 5) * 8 + (target & 7)
    match = jnp.where((names == target) & live, 1.0, 0.0)
    before = jnp.where(
        lax.broadcasted_iota(jnp.int32, (256, 256), 0) < lax.broadcasted_iota(jnp.int32, (256, 256), 1), 1.0, 0.0
    ).astype(BF16)
    rank = dot(match.astype(BF16), before)
    for k in range(CAP):
        sel[pl.ds(128 * k, 128), :] = jnp.where(rank == k, match, 0.0).astype(BF16)
    w = w_v[...]
    portion = w / jnp.sum(w, axis=1, keepdims=True)
    high, mid = split2(portion)
    for k in range(CAP):
        pick = sel[pl.ds(128 * k, 128), :]
        rows = dot(pick, high) + dot(pick, mid)
        sb[pl.ds(2 * k, 128, stride=8), :] = rows[:, :128]
        sb[pl.ds(2 * k + 1, 128, stride=8), :] = rows[:, 128:]

    for load in loads[3:6]:
        load.wait()
    lives = [lax.broadcasted_iota(jnp.int32, (1, 128), 1) + 128 * half < count for half in range(2)]
    for j in range(8):
        half, f = j // 4, j % 4
        rows = pl.ds(512 * half + f, 128, stride=4)
        pm[pl.ds(j, 128, stride=8), :] = rhiz_v[rows, :].T
        cm[pl.ds(j, 128, stride=8), :] = jnp.where(lives[half], cond_v[rows, :].T, 0.0)
    uptake = jnp.concatenate(
        [jnp.where(lives[half], upt_v[:, pl.ds(128 * half, 128)], 0.0) for half in range(2)], axis=0
    )

    zero, one = jnp.zeros((8, 128), F32), jnp.ones((8, 128), F32)
    for r in range(NR - 32, NR):
        tm[row(r), :] = pm[row(r), :]
        um[row(r), :] = zero
    drawn0, gain = zero, zero
    for g in range(4):
        drawn0 = lax.fori_loop(0, 4, lambda i, d, g=g: d + double_step(tm, cm, NR - 32 + 8 * g, zero, None), drawn0)
        gain = lax.fori_loop(0, 4, lambda i, d, g=g: d + double_step(um, cm, NR - 8 - 8 * g, one, None), gain)

    def as_rows(v):
        return jnp.concatenate([v[0:4], v[4:8]], axis=1)

    tile_row = tile_v[...].astype(F32)
    items = jnp.concatenate(
        [tile_row, jnp.zeros((3, 256), F32), as_rows(drawn0), as_rows(gain), jnp.zeros((4, 256), F32)], axis=0
    )
    meta = jnp.zeros((128, 128), F32)
    for k in range(CAP):
        parts = [jnp.zeros((32 * k, 256), F32)] if k else []
        wide = jnp.concatenate(parts + [items, jnp.zeros((112 - 32 * k, 256), F32)], axis=0)
        pick = sel[pl.ds(128 * k, 128), :]
        for piece in split3(wide):
            meta = meta + dot(pick, piece, NT)
    sb[pl.ds(6, 128, stride=8), :] = meta


    loads[6].wait()
    soil = jnp.concatenate(
        [
            jnp.concatenate([soil_v[pl.ds(4 * half + f, 64, stride=8), :] for half in range(2)], axis=1)
            for f in range(4)
        ],
        axis=0,
    )
    soil_high, soil_mid = split2(soil)
    tiles = (lax.broadcasted_iota(jnp.int32, (256, 128), 0) & 63).astype(F32)

    def arrived(p):
        blank = [jnp.zeros((32, 128), F32)]
        halves = [[rb[pl.ds(256 * p + 2 * k + half, 32, stride=8), :] for k in range(CAP)] for half in range(2)]
        return split2(jnp.concatenate([jnp.concatenate(half + blank, axis=0) for half in halves], axis=1))

    @pl.when(z < 0)
    def _():
        lax.fori_loop(0, SUB // 2, lambda i, d: d + double_step(pm, cm, 0, zero, uptake), zero)

    pl.semaphore_wait(barrier, len(PLANE) + 3)
    for dz in (2, 1, 3):
        pl.semaphore_signal(plane_sem.at[z], inc=1, device_id=device(x, y, (z + dz) & 3, c), device_id_type=MESH)

    def give(p):
        @pl.when(z != p)
        def _():
            pl.semaphore_wait(plane_sem.at[p], 1)

        send(p, sb, rb, send_sem, recv_sem, block)

    def answer(p):
        view = rb.at[pl.ds(0, 32 * MESSAGE), :]
        pltpu.make_async_copy(view, view, recv_sem.at[p]).wait()
        high, mid = arrived(p)
        field = dot(soil_high, high, NT) + dot(soil_high, mid, NT) + dot(soil_mid, high, NT)
        items = rb[pl.ds(256 * p + 6, 32, stride=8), :]
        info = jnp.concatenate(
            [items, pltpu.roll(items, 96, 1), pltpu.roll(items, 64, 1), jnp.full((32, 128), -1.0, F32)], axis=0
        ).T
        masked = jnp.where(tiles == info[0:1], field, 0.0)
        values = [jnp.sum(masked[64 * f : 64 * f + 64], axis=0, keepdims=True) for f in range(4)]
        reply = jnp.concatenate(values + [jnp.zeros((124, 128), F32)], axis=0).T
        qb[pl.ds(32 * p, 32), 0, :] = reply[0:32] + pltpu.roll(reply[32:64], 8, 1) + pltpu.roll(reply[64:96], 16, 1)
        send(p, qb, ret, send2_sem, recv2_sem, lambda r: r)
        info_v[pl.ds(24 * p, 24), :] = jnp.concatenate([info[0:12]] + values + [jnp.zeros((8, 128), F32)], axis=0)

    @pl.when(z == 9)
    def _():
        for p in range(4):
            give(p)
            answer(p)

    @pl.when(jnp.logical_not(z == 9))
    def _():
        for p in (0, 1, 2, 3):
            give(p)
        for p in range(4):
            answer(p)

    sink = jnp.zeros((256, 256), F32)
    for p in range(4):
        info = info_v[pl.ds(24 * p, 24), :]
        drawn = info[4:8] + info[8:12] * info[12:16]
        spread = jnp.concatenate([jnp.broadcast_to(drawn[f : f + 1], (64, 128)) for f in range(4)], axis=0)
        share_high, share_mid = split2(jnp.where(tiles == info[0:1], spread, 0.0))
        high, mid = arrived(p)
        sink = sink + dot(share_high, high) + dot(share_high, mid) + dot(share_mid, high)
    for f in range(4):
        for half in range(2):
            sink_v[pl.ds(4 * half + f, 64, stride=8), :] = sink[64 * f : 64 * f + 64, 128 * half : 128 * half + 128]
    outs = [
        pltpu.make_async_copy(s, d, out_sems.at[i])
        for i, (s, d) in enumerate([(sink_v, sink_o), (pm, pm_o), (um.at[pl.ds(8 * (NR - 32), 256), :], um_o), (sel, sel_o)])
    ]
    outs[0].start()
    outs[2].start()
    outs[3].start()
    lax.fori_loop(0, 16, lambda i, d: d + double_step(pm, cm, 0, zero, uptake), zero)
    outs[1].start()

    for p in range(4):
        view = ret.at[pl.ds(0, 32)]
        pltpu.make_async_copy(view, view, recv2_sem.at[p]).wait()
    view = sb.at[pl.ds(0, 127 * MESSAGE), :]
    pltpu.make_async_copy(view, view, send_sem).wait()
    view = qb.at[pl.ds(0, 127)]
    pltpu.make_async_copy(view, view, send2_sem).wait()
    for out in outs:
        out.wait()


def finish(pm_h, um_h, sel_h, sink_h, ret_h, next_o, sink_o, pm, um, sel, ret, next_v, sink_v, in_sems, out_sems):
    sink_copy = pltpu.make_async_copy(sink_v, sink_o, out_sems.at[2])
    loads = [
        pltpu.make_async_copy(s, d, in_sems.at[i])
        for i, (s, d) in enumerate([(ret_h, ret), (sel_h, sel), (um_h, um), (pm_h, pm), (sink_h, sink_v)])
    ]
    for load in loads:
        load.start()
    loads[0].wait()
    loads[1].wait()
    back = ret[...].T
    bound = jnp.zeros((8, 256), F32)
    for k in range(CAP):
        pick = sel[pl.ds(128 * k, 128), :]
        for piece in split3(back[8 * k : 8 * k + 8]):
            bound = bound + dot(piece, pick)
    bound = jnp.concatenate([bound[0:4, :128], bound[0:4, 128:]], axis=0)
    loads[4].wait()
    sink_copy.start()
    loads[2].wait()
    loads[3].wait()
    for r in range(32):
        at = row(NR - 32 + r)
        pm[at, :] = pm[at, :] + bound * um[row(r), :]
    for half in range(2):
        for f in range(4):
            next_v[pl.ds(512 * half + f, 128, stride=4), :] = pm[pl.ds(4 * half + f, 128, stride=8), :].T
        rows = pl.ds(512 * half, 512)
        pltpu.make_async_copy(next_v.at[rows, :], next_o.at[rows, :], out_sems.at[half]).start()
    for half in range(2):
        rows = pl.ds(512 * half, 512)
        pltpu.make_async_copy(next_v.at[rows, :], next_o.at[rows, :], out_sems.at[half]).wait()
    sink_copy.wait()


def on_device(
    soil_field, rhizosphere, conductance, uptake_rate, segment_weight, segment_target, segment_tile, segment_count
):
    soil = soil_field.reshape(64, 4, 2, 128).transpose(0, 2, 1, 3).reshape(512, 128)
    vm, dma = pltpu.VMEM, pltpu.SemaphoreType.DMA
    any_spec = pl.BlockSpec(memory_space=pl.ANY)
    pm, um, sel, sink, ret = pl.pallas_call(
        exchange,
        out_shape=(
            jax.ShapeDtypeStruct((1024, 128), F32), jax.ShapeDtypeStruct((256, 128), F32),
            jax.ShapeDtypeStruct((384, 256), BF16), jax.ShapeDtypeStruct((512, 128), F32),
            jax.ShapeDtypeStruct((128, 1, 128), F32),
        ),
        in_specs=[any_spec] * 7 + [pl.BlockSpec(memory_space=pltpu.SMEM)],
        out_specs=(any_spec,) * 5,
        scratch_shapes=[
            vm((512, 128), F32), vm((1024, 128), F32), vm((1024, 128), F32), vm((4, 256), F32), vm((256, 256), F32),
            vm((1, 256), jnp.int32), vm((1, 256), jnp.int32), vm((512, 128), F32),
            vm((1024, 128), F32), vm((1024, 128), F32), vm((1024, 128), F32), vm((1024, 128), F32),
            vm((384, 256), BF16), vm((1024, 128), F32), vm((1024, 128), F32), vm((128, 1, 128), F32), vm((96, 128), F32),
            dma((7,)), dma((4,)), pltpu.SemaphoreType.REGULAR((4,)), dma(()), dma((4,)), dma(()), dma((4,)),
        ],
        compiler_params=pltpu.CompilerParams(
            collective_id=0, has_side_effects=True, vmem_limit_bytes=60 * 1024 * 1024
        ),
    )(
        soil,
        rhizosphere.reshape(1024, 128),
        conductance.reshape(1024, 128),
        uptake_rate.T,
        segment_weight,
        segment_target.reshape(1, 256),
        segment_tile.reshape(1, 256),
        segment_count,
    )
    nxt, sink = pl.pallas_call(
        finish,
        out_shape=(jax.ShapeDtypeStruct((1024, 128), F32), jax.ShapeDtypeStruct((512, 128), F32)),
        in_specs=[any_spec] * 5,
        out_specs=(any_spec,) * 2,
        scratch_shapes=[
            vm((1024, 128), F32), vm((256, 128), F32), vm((384, 256), BF16), vm((128, 128), F32), vm((1024, 128), F32), vm((512, 128), F32),
            dma((5,)), dma((3,)),
        ],
        compiler_params=pltpu.CompilerParams(vmem_limit_bytes=60 * 1024 * 1024),
    )(pm, um, sel, sink, ret.reshape(128, 128))
    sink = sink.reshape(64, 2, 4, 128).transpose(0, 2, 1, 3)
    return nxt.reshape(256, 4, 128), sink.reshape(8, 8, 4, 256)


def solution(mesh):
    flat = ("gx", "gy")
    return jax.shard_map(
        on_device,
        mesh=mesh,
        in_specs=(
            P("gx", "gy", None, None), P(flat, None, None), P(flat, None, None), P(flat, None), P(flat, None),
            P(flat, None), P(flat), P(flat),
        ),
        out_specs=(P(flat, None, None), P("gx", "gy", None, None)),
        check_vma=False,
    )
```

```python
import itertools

import jax
import jax.numpy as jnp
from jax import lax
from jax.experimental import pallas as pl
from jax.experimental.pallas import tpu as pltpu
from jax.sharding import PartitionSpec as P

SUB = 32
CAP = 3
NR = 128
F32 = jnp.float32
BF16 = jnp.bfloat16
MESH = pl.DeviceIdType.MESH
NN = (((1,), (0,)), ((), ()))
NT = (((1,), (1,)), ((), ()))


MESSAGE = 7


def hops(o):
    return sum(min(v, 4 - v) for v in o[:2])


PLANE = sorted((o for o in itertools.product(range(4), range(4), range(2)) if any(o)), key=lambda o: (-hops(o), o))


def coords():
    gx, gy = lax.axis_index("gx"), lax.axis_index("gy")
    return gy // 2, gx // 4, lax.rem(gx, 4), lax.rem(gy, 2)


def device(x, y, z, c):
    return y * 4 + z, x * 2 + c


def place(x, y, z, c):
    return z * 32 + y * 8 + x * 2 + c


def dot(a, b, dims=NN):
    return lax.dot_general(a, b, dims, preferred_element_type=F32)


def split2(x):
    high = x.astype(BF16)
    return high, (x - high.astype(F32)).astype(BF16)


def split3(x):
    high, mid = split2(x)
    return high, mid, (x - high.astype(F32) - mid.astype(F32)).astype(BF16)


def row(r):
    return pl.ds(8 * r, 8)


def double_step(level, cond, low, boundary, uptake):
    l0 = level[row(low), :]
    zero = jnp.zeros((8, 128), F32)
    p0 = uptake * l0 if uptake is not None else zero
    p1 = l1 = cp = None
    for r in range(low, NR):
        c = cond[row(r), :]
        outer = level[row(r + 1), :] if r < NR - 1 else boundary
        cur = c * (outer - l0)
        new = l0 + cur - p0 if p0 is not None else l0 + cur
        p0, l0 = cur, outer
        if r == low:
            p1 = uptake * new if uptake is not None else zero
        else:
            cur1 = cp * (new - l1)
            level[row(r - 1), :] = l1 + cur1 - p1
            p1 = cur1
        l1, cp = new, c
    cur1 = cp * (boundary - l1)
    level[row(NR - 1), :] = l1 + cur1 - p1
    return p0 + cur1


def exchange(
    soil_h, rhiz_h, cond_h, upt_h, w_h, tgt_h, tile_h, cnt_s,
    pm, um, sel, sink_v, ret,
    soil_v, rhiz_v, cond_v, upt_v, w_v, tgt_v, tile_v,
    cm, tm, sb, rb, qb, info_v,
    in_sems, plane_sem, send_sem, recv_sem, send2_sem, recv2_sem,
):
    x, y, z, c = coords()
    me = place(x, y, z, c)
    loads = [
        pltpu.make_async_copy(s, d, in_sems.at[i])
        for i, (s, d) in enumerate(
            [(tgt_h, tgt_v), (tile_h, tile_v), (w_h, w_v), (cond_h, cond_v), (rhiz_h, rhiz_v), (upt_h, upt_v), (soil_h, soil_v)]
        )
    ]

    def beside(o):
        return (x + o[0]) & 3, (y + o[1]) & 3, c ^ o[2]

    barrier = pltpu.get_barrier_semaphore()
    for dz in (2, 1, 3):
        pl.semaphore_signal(barrier, inc=1, device_id=device(x, y, (z + dz) & 3, c), device_id_type=MESH)
    for o in PLANE:
        ox, oy, oc = beside(o)
        pl.semaphore_signal(barrier, inc=1, device_id=device(ox, oy, z, oc), device_id_type=MESH)
    for load in loads:
        load.start()
    count = cnt_s[0]

    def send(p, src, dst, send_s, recv_s, rows):
        def copy_to(x, y, c):
            there = place(x, y, p, c)
            return pltpu.make_async_remote_copy(
                src.at[rows(there)], dst.at[rows(me)], send_s, recv_s.at[z],
                device_id=device(x, y, p, c), device_id_type=MESH,
            )

        for o in PLANE:
            copy_to(*beside(o)).start()

        @pl.when(z != p)
        def _():
            copy_to(x, y, c).start()

        @pl.when(z == p)
        def _():
            pltpu.make_async_copy(src.at[rows(me)], dst.at[rows(me)], recv_s.at[z]).start()

    def block(r):
        return pl.ds(8 * r, MESSAGE)

    for load in loads[:3]:
        load.wait()
    live = lax.broadcasted_iota(jnp.int32, (1, 256), 1) < count
    names = lax.broadcasted_iota(jnp.int32, (128, 256), 0)
    target = tgt_v[...]
    target = ((target >> 3) & 3) * 32 + (target >> 5) * 8 + (target & 7)
    match = jnp.where((names == target) & live, 1.0, 0.0)
    before = jnp.where(
        lax.broadcasted_iota(jnp.int32, (256, 256), 0) < lax.broadcasted_iota(jnp.int32, (256, 256), 1), 1.0, 0.0
    ).astype(BF16)
    rank = dot(match.astype(BF16), before)
    for k in range(CAP):
        sel[pl.ds(128 * k, 128), :] = jnp.where(rank == k, match, 0.0).astype(BF16)
    w = w_v[...]
    portion = w / jnp.sum(w, axis=1, keepdims=True)
    high, mid = split2(portion)
    for k in range(CAP):
        pick = sel[pl.ds(128 * k, 128), :]
        rows = dot(pick, high) + dot(pick, mid)
        sb[pl.ds(2 * k, 128, stride=8), :] = rows[:, :128]
        sb[pl.ds(2 * k + 1, 128, stride=8), :] = rows[:, 128:]

    for load in loads[3:6]:
        load.wait()
    lives = [lax.broadcasted_iota(jnp.int32, (1, 128), 1) + 128 * half < count for half in range(2)]
    for j in range(8):
        half, f = j // 4, j % 4
        rows = pl.ds(512 * half + f, 128, stride=4)
        pm[pl.ds(j, 128, stride=8), :] = rhiz_v[rows, :].T
        cm[pl.ds(j, 128, stride=8), :] = jnp.where(lives[half], cond_v[rows, :].T, 0.0)
    uptake = jnp.concatenate(
        [jnp.where(lives[half], upt_v[:, pl.ds(128 * half, 128)], 0.0) for half in range(2)], axis=0
    )

    def tell():
        pl.semaphore_wait(barrier, len(PLANE) + 3)
        for dz in (2, 1, 3):
            pl.semaphore_signal(plane_sem.at[z], inc=1, device_id=device(x, y, (z + dz) & 3, c), device_id_type=MESH)

    late = (x >= 2) & (y >= 2) & (z >= 2)
    pl.when(late)(tell)

    zero, one = jnp.zeros((8, 128), F32), jnp.ones((8, 128), F32)
    for r in range(NR - 32, NR):
        tm[row(r), :] = pm[row(r), :]
        um[row(r), :] = zero
    drawn0, gain = zero, zero
    for g in range(4):
        drawn0 = lax.fori_loop(0, 4, lambda i, d, g=g: d + double_step(tm, cm, NR - 32 + 8 * g, zero, None), drawn0)
        gain = lax.fori_loop(0, 4, lambda i, d, g=g: d + double_step(um, cm, NR - 8 - 8 * g, one, None), gain)

    def as_rows(v):
        return jnp.concatenate([v[0:4], v[4:8]], axis=1)

    tile_row = tile_v[...].astype(F32)
    items = jnp.concatenate(
        [tile_row, jnp.zeros((3, 256), F32), as_rows(drawn0), as_rows(gain), jnp.zeros((4, 256), F32)], axis=0
    )
    meta = jnp.zeros((128, 128), F32)
    for k in range(CAP):
        parts = [jnp.zeros((32 * k, 256), F32)] if k else []
        wide = jnp.concatenate(parts + [items, jnp.zeros((112 - 32 * k, 256), F32)], axis=0)
        pick = sel[pl.ds(128 * k, 128), :]
        for piece in split3(wide):
            meta = meta + dot(pick, piece, NT)
    sb[pl.ds(6, 128, stride=8), :] = meta


    loads[6].wait()
    soil = jnp.concatenate(
        [
            jnp.concatenate([soil_v[pl.ds(4 * half + f, 64, stride=8), :] for half in range(2)], axis=1)
            for f in range(4)
        ],
        axis=0,
    )
    soil_high, soil_mid = split2(soil)
    tiles = (lax.broadcasted_iota(jnp.int32, (256, 128), 0) & 63).astype(F32)

    def arrived(p):
        blank = [jnp.zeros((32, 128), F32)]
        halves = [[rb[pl.ds(256 * p + 2 * k + half, 32, stride=8), :] for k in range(CAP)] for half in range(2)]
        return split2(jnp.concatenate([jnp.concatenate(half + blank, axis=0) for half in halves], axis=1))

    pl.when(jnp.logical_not(late))(tell)

    def give(p):
        @pl.when(z != p)
        def _():
            pl.semaphore_wait(plane_sem.at[p], 1)

        send(p, sb, rb, send_sem, recv_sem, block)

    def answer(p):
        view = rb.at[pl.ds(0, 32 * MESSAGE), :]
        pltpu.make_async_copy(view, view, recv_sem.at[p]).wait()
        high, mid = arrived(p)
        field = dot(soil_high, high, NT) + dot(soil_high, mid, NT) + dot(soil_mid, high, NT)
        items = rb[pl.ds(256 * p + 6, 32, stride=8), :]
        info = jnp.concatenate(
            [items, pltpu.roll(items, 96, 1), pltpu.roll(items, 64, 1), jnp.full((32, 128), -1.0, F32)], axis=0
        ).T
        masked = jnp.where(tiles == info[0:1], field, 0.0)
        values = [jnp.sum(masked[64 * f : 64 * f + 64], axis=0, keepdims=True) for f in range(4)]
        reply = jnp.concatenate(values + [jnp.zeros((124, 128), F32)], axis=0).T
        qb[pl.ds(32 * p, 32), 0, :] = reply[0:32] + pltpu.roll(reply[32:64], 8, 1) + pltpu.roll(reply[64:96], 16, 1)
        send(p, qb, ret, send2_sem, recv2_sem, lambda r: r)
        info_v[pl.ds(24 * p, 24), :] = jnp.concatenate([info[0:12]] + values + [jnp.zeros((8, 128), F32)], axis=0)

    for p in range(4):
        give(p)
    for p in range(4):
        answer(p)

    sink = jnp.zeros((256, 256), F32)
    for p in range(4):
        info = info_v[pl.ds(24 * p, 24), :]
        drawn = info[4:8] + info[8:12] * info[12:16]
        spread = jnp.concatenate([jnp.broadcast_to(drawn[f : f + 1], (64, 128)) for f in range(4)], axis=0)
        share_high, share_mid = split2(jnp.where(tiles == info[0:1], spread, 0.0))
        high, mid = arrived(p)
        sink = sink + dot(share_high, high) + dot(share_high, mid) + dot(share_mid, high)
    for f in range(4):
        for half in range(2):
            sink_v[pl.ds(4 * half + f, 64, stride=8), :] = sink[64 * f : 64 * f + 64, 128 * half : 128 * half + 128]
    lax.fori_loop(0, SUB // 2, lambda i, d: d + double_step(pm, cm, 0, zero, uptake), zero)

    for p in range(4):
        view = ret.at[pl.ds(0, 32)]
        pltpu.make_async_copy(view, view, recv2_sem.at[p]).wait()
    view = sb.at[pl.ds(0, 127 * MESSAGE), :]
    pltpu.make_async_copy(view, view, send_sem).wait()
    view = qb.at[pl.ds(0, 127)]
    pltpu.make_async_copy(view, view, send2_sem).wait()


def finish(pm, um, sel, sink, ret, next_o, sink_o, last, next_v, out_sems):
    sink_copy = pltpu.make_async_copy(sink, sink_o, out_sems.at[2])
    sink_copy.start()
    back = jnp.concatenate(split2(ret[:, 0, :].T[0:32]), axis=0)
    bound = jnp.zeros((8, 256), F32)
    for k in range(CAP):
        part = dot(back, sel[pl.ds(128 * k, 128), :])
        bound = bound + part[8 * k : 8 * k + 8] + part[32 + 8 * k : 40 + 8 * k]
    bound = jnp.concatenate([bound[0:4, :128], bound[0:4, 128:]], axis=0)
    for r in range(NR - 32, NR):
        last[row(r - NR + 32), :] = pm[row(r), :] + bound * um[row(r), :]
    for half in range(2):
        for f in range(4):
            j = 4 * half + f
            block = jnp.concatenate(
                [pm[pl.ds(j, NR - 32, stride=8), :], last[pl.ds(j, 32, stride=8), :]], axis=0
            )
            next_v[pl.ds(512 * half + f, 128, stride=4), :] = block.T
        rows = pl.ds(512 * half, 512)
        pltpu.make_async_copy(next_v.at[rows, :], next_o.at[rows, :], out_sems.at[half]).start()
    for half in range(2):
        rows = pl.ds(512 * half, 512)
        pltpu.make_async_copy(next_v.at[rows, :], next_o.at[rows, :], out_sems.at[half]).wait()
    sink_copy.wait()


def on_device(
    soil_field, rhizosphere, conductance, uptake_rate, segment_weight, segment_target, segment_tile, segment_count
):
    soil = soil_field.reshape(64, 4, 2, 128).transpose(0, 2, 1, 3).reshape(512, 128)
    vm, dma = pltpu.VMEM, pltpu.SemaphoreType.DMA
    any_spec, vmem_spec = pl.BlockSpec(memory_space=pl.ANY), pl.BlockSpec(memory_space=pltpu.VMEM)

    def hbm(a):
        return pltpu.with_memory_space_constraint(a, pltpu.HBM)

    pm, um, sel, sink, ret = pl.pallas_call(
        exchange,
        out_shape=(
            vm((1024, 128), F32), vm((1024, 128), F32), vm((384, 256), BF16), vm((512, 128), F32), vm((128, 1, 128), F32),
        ),
        in_specs=[any_spec] * 7 + [pl.BlockSpec(memory_space=pltpu.SMEM)],
        out_specs=(vmem_spec,) * 5,
        scratch_shapes=[
            vm((512, 128), F32), vm((1024, 128), F32), vm((1024, 128), F32), vm((4, 256), F32), vm((256, 256), F32),
            vm((1, 256), jnp.int32), vm((1, 256), jnp.int32), vm((1024, 128), F32), vm((1024, 128), F32),
            vm((1024, 128), F32), vm((1024, 128), F32), vm((128, 1, 128), F32), vm((96, 128), F32),
            dma((7,)), pltpu.SemaphoreType.REGULAR((4,)), dma(()), dma((4,)), dma(()), dma((4,)),
        ],
        compiler_params=pltpu.CompilerParams(
            collective_id=0, has_side_effects=True, vmem_limit_bytes=32 * 1024 * 1024
        ),
    )(
        hbm(soil),
        hbm(rhizosphere.reshape(1024, 128)),
        hbm(conductance.reshape(1024, 128)),
        hbm(uptake_rate.T),
        hbm(segment_weight),
        hbm(segment_target.reshape(1, 256)),
        hbm(segment_tile.reshape(1, 256)),
        segment_count,
    )
    nxt, sink = pl.pallas_call(
        finish,
        out_shape=(jax.ShapeDtypeStruct((1024, 128), F32), jax.ShapeDtypeStruct((512, 128), F32)),
        in_specs=[vmem_spec] * 5,
        out_specs=(any_spec,) * 2,
        scratch_shapes=[vm((256, 128), F32), vm((1024, 128), F32), dma((3,))],
        compiler_params=pltpu.CompilerParams(vmem_limit_bytes=16 * 1024 * 1024),
    )(*(pltpu.with_memory_space_constraint(a, pltpu.VMEM) for a in (pm, um, sel, sink, ret)))
    sink = sink.reshape(64, 2, 4, 128).transpose(0, 2, 1, 3)
    return nxt.reshape(256, 4, 128), sink.reshape(8, 8, 4, 256)


def solution(mesh):
    flat = ("gx", "gy")
    return jax.shard_map(
        on_device,
        mesh=mesh,
        in_specs=(
            P("gx", "gy", None, None), P(flat, None, None), P(flat, None, None), P(flat, None), P(flat, None),
            P(flat, None), P(flat), P(flat),
        ),
        out_specs=(P(flat, None, None), P("gx", "gy", None, None)),
        check_vma=False,
    )
```

```python
import itertools

import jax
import jax.numpy as jnp
from jax import lax
from jax.experimental import pallas as pl
from jax.experimental.pallas import tpu as pltpu
from jax.sharding import PartitionSpec as P

SUB = 32
CAP = 3
NR = 128
F32 = jnp.float32
BF16 = jnp.bfloat16
MESH = pl.DeviceIdType.MESH
NN = (((1,), (0,)), ((), ()))
NT = (((1,), (1,)), ((), ()))


MESSAGE = 7


def hops(o):
    return sum(min(v, 4 - v) for v in o[:2])


PLANE = sorted((o for o in itertools.product(range(4), range(4), range(2)) if any(o)), key=lambda o: (-hops(o), o))


def coords():
    gx, gy = lax.axis_index("gx"), lax.axis_index("gy")
    return gy // 2, gx // 4, lax.rem(gx, 4), lax.rem(gy, 2)


def device(x, y, z, c):
    return y * 4 + z, x * 2 + c


def place(x, y, z, c):
    return z * 32 + y * 8 + x * 2 + c


def dot(a, b, dims=NN):
    return lax.dot_general(a, b, dims, preferred_element_type=F32)


def split2(x):
    high = x.astype(BF16)
    return high, (x - high.astype(F32)).astype(BF16)


def split3(x):
    high, mid = split2(x)
    return high, mid, (x - high.astype(F32) - mid.astype(F32)).astype(BF16)


def row(r):
    return pl.ds(8 * r, 8)


def double_step(level, cond, low, boundary, uptake):
    l0 = level[row(low), :]
    zero = jnp.zeros((8, 128), F32)
    p0 = uptake * l0 if uptake is not None else zero
    p1 = l1 = cp = None
    for r in range(low, NR):
        c = cond[row(r), :]
        outer = level[row(r + 1), :] if r < NR - 1 else boundary
        cur = c * (outer - l0)
        new = l0 + cur - p0 if p0 is not None else l0 + cur
        p0, l0 = cur, outer
        if r == low:
            p1 = uptake * new if uptake is not None else zero
        else:
            cur1 = cp * (new - l1)
            level[row(r - 1), :] = l1 + cur1 - p1
            p1 = cur1
        l1, cp = new, c
    cur1 = cp * (boundary - l1)
    level[row(NR - 1), :] = l1 + cur1 - p1
    return p0 + cur1


def exchange(
    soil_h, rhiz_h, cond_h, upt_h, w_h, tgt_h, tile_h, cnt_s,
    pm, um, sel, sink_v, ret,
    soil_v, rhiz_v, cond_v, upt_v, w_v, tgt_v, tile_v,
    cm, tm, sb, rb, qb, info_v,
    in_sems, plane_sem, send_sem, recv_sem, send2_sem, recv2_sem,
):
    x, y, z, c = coords()
    me = place(x, y, z, c)
    loads = [
        pltpu.make_async_copy(s, d, in_sems.at[i])
        for i, (s, d) in enumerate(
            [(tgt_h, tgt_v), (tile_h, tile_v), (w_h, w_v), (cond_h, cond_v), (rhiz_h, rhiz_v), (upt_h, upt_v), (soil_h, soil_v)]
        )
    ]

    def beside(o):
        return (x + o[0]) & 3, (y + o[1]) & 3, c ^ o[2]

    barrier = pltpu.get_barrier_semaphore()
    for o in PLANE:
        ox, oy, oc = beside(o)
        pl.semaphore_signal(barrier, inc=1, device_id=device(ox, oy, z, oc), device_id_type=MESH)
    for load in loads:
        load.start()
    count = cnt_s[0]

    def send(p, src, dst, send_s, recv_s, rows):
        def copy_to(x, y, c):
            there = place(x, y, p, c)
            return pltpu.make_async_remote_copy(
                src.at[rows(there)], dst.at[rows(me)], send_s, recv_s,
                device_id=device(x, y, p, c), device_id_type=MESH,
            )

        for o in PLANE:
            copy_to(*beside(o)).start()

        @pl.when(z != p)
        def _():
            copy_to(x, y, c).start()

        @pl.when(z == p)
        def _():
            pltpu.make_async_copy(src.at[rows(me)], dst.at[rows(me)], recv_s).start()

    def block(r):
        return pl.ds(8 * r, MESSAGE)

    for load in loads[:3]:
        load.wait()
    live = lax.broadcasted_iota(jnp.int32, (1, 256), 1) < count
    names = lax.broadcasted_iota(jnp.int32, (128, 256), 0)
    target = tgt_v[...]
    target = ((target >> 3) & 3) * 32 + (target >> 5) * 8 + (target & 7)
    match = jnp.where((names == target) & live, 1.0, 0.0)
    before = jnp.where(
        lax.broadcasted_iota(jnp.int32, (256, 256), 0) < lax.broadcasted_iota(jnp.int32, (256, 256), 1), 1.0, 0.0
    ).astype(BF16)
    rank = dot(match.astype(BF16), before)
    for k in range(CAP):
        sel[pl.ds(128 * k, 128), :] = jnp.where(rank == k, match, 0.0).astype(BF16)
    w = w_v[...]
    portion = w / jnp.sum(w, axis=1, keepdims=True)
    high, mid = split2(portion)
    for k in range(CAP):
        pick = sel[pl.ds(128 * k, 128), :]
        rows = dot(pick, high) + dot(pick, mid)
        sb[pl.ds(2 * k, 128, stride=8), :] = rows[:, :128]
        sb[pl.ds(2 * k + 1, 128, stride=8), :] = rows[:, 128:]

    for load in loads[3:6]:
        load.wait()
    lives = [lax.broadcasted_iota(jnp.int32, (1, 128), 1) + 128 * half < count for half in range(2)]
    for j in range(8):
        half, f = j // 4, j % 4
        rows = pl.ds(512 * half + f, 128, stride=4)
        pm[pl.ds(j, 128, stride=8), :] = rhiz_v[rows, :].T
        cm[pl.ds(j, 128, stride=8), :] = jnp.where(lives[half], cond_v[rows, :].T, 0.0)
    uptake = jnp.concatenate(
        [jnp.where(lives[half], upt_v[:, pl.ds(128 * half, 128)], 0.0) for half in range(2)], axis=0
    )

    def tell():
        pl.semaphore_wait(barrier, len(PLANE) + z)
        for dz in (1, 2, 3):

            @pl.when(z >= dz)
            def _():
                pl.semaphore_signal(plane_sem.at[z], inc=1, device_id=device(x, y, z - dz, c), device_id_type=MESH)

            @pl.when(z + dz < 4)
            def _():
                pl.semaphore_signal(barrier, inc=1, device_id=device(x, y, z + dz, c), device_id_type=MESH)

    late = (x >= 1) & (y >= 1)
    pl.when(late)(tell)

    zero, one = jnp.zeros((8, 128), F32), jnp.ones((8, 128), F32)
    for r in range(NR - 32, NR):
        tm[row(r), :] = pm[row(r), :]
        um[row(r), :] = zero
    drawn0, gain = zero, zero
    for g in range(4):
        drawn0 = lax.fori_loop(0, 4, lambda i, d, g=g: d + double_step(tm, cm, NR - 32 + 8 * g, zero, None), drawn0)
        gain = lax.fori_loop(0, 4, lambda i, d, g=g: d + double_step(um, cm, NR - 8 - 8 * g, one, None), gain)

    def as_rows(v):
        return jnp.concatenate([v[0:4], v[4:8]], axis=1)

    tile_row = tile_v[...].astype(F32)
    items = jnp.concatenate(
        [tile_row, jnp.zeros((3, 256), F32), as_rows(drawn0), as_rows(gain), jnp.zeros((4, 256), F32)], axis=0
    )
    meta = jnp.zeros((128, 128), F32)
    for k in range(CAP):
        parts = [jnp.zeros((32 * k, 256), F32)] if k else []
        wide = jnp.concatenate(parts + [items, jnp.zeros((112 - 32 * k, 256), F32)], axis=0)
        pick = sel[pl.ds(128 * k, 128), :]
        for piece in split3(wide):
            meta = meta + dot(pick, piece, NT)
    sb[pl.ds(6, 128, stride=8), :] = meta


    loads[6].wait()
    soil = jnp.concatenate(
        [
            jnp.concatenate([soil_v[pl.ds(4 * half + f, 64, stride=8), :] for half in range(2)], axis=1)
            for f in range(4)
        ],
        axis=0,
    )
    soil_high, soil_mid = split2(soil)
    tiles = (lax.broadcasted_iota(jnp.int32, (256, 128), 0) & 63).astype(F32)

    def arrived(p):
        blank = [jnp.zeros((32, 128), F32)]
        halves = [[rb[pl.ds(256 * p + 2 * k + half, 32, stride=8), :] for k in range(CAP)] for half in range(2)]
        return split2(jnp.concatenate([jnp.concatenate(half + blank, axis=0) for half in halves], axis=1))

    def whole():
        lax.fori_loop(0, SUB // 2, lambda i, d: d + double_step(pm, cm, 0, zero, uptake), zero)

    @pl.when((z == 0) & (x < 2) & (y < 2))
    def _():
        whole()

    pl.when(jnp.logical_not(late))(tell)

    def give(p):
        @pl.when(z < p)
        def _():
            pl.semaphore_wait(plane_sem.at[p], 1)

        send(p, sb, rb, send_sem, recv_sem.at[2 * z + jnp.minimum(y, 1)], block)

    def take(p, part):
        view = rb.at[pl.ds(0, (8, 24)[part] * MESSAGE), :]
        pltpu.make_async_copy(view, view, recv_sem.at[2 * p + part]).wait()

    def values_of(info, high, mid):
        field = dot(soil_high, high, NT) + dot(soil_high, mid, NT) + dot(soil_mid, high, NT)
        masked = jnp.where(tiles == info[0:1], field, 0.0)
        return [jnp.sum(masked[64 * f : 64 * f + 64], axis=0, keepdims=True) for f in range(4)]

    def items_of(start, n):
        items = rb[pl.ds(start + 6, n, stride=8), :]
        rest = jnp.full((128 - 3 * n, 128), -1.0, F32)
        return jnp.concatenate([items, pltpu.roll(items, 96, 1), pltpu.roll(items, 64, 1), rest], axis=0).T

    def by_source(values, n):
        reply = jnp.concatenate(values + [jnp.zeros((124, 128), F32)], axis=0).T
        return reply[0:n] + pltpu.roll(reply[n : 2 * n], 8, 1) + pltpu.roll(reply[2 * n : 3 * n], 16, 1)

    def reply_to(y_there):
        for x_there in (0, 1, 3, 2):
            for c_there in range(2):
                there = place(x_there, y_there, 0, c_there)
                pltpu.make_async_remote_copy(
                    qb.at[there], ret.at[me], send2_sem, recv2_sem.at[z],
                    device_id=device(x_there, y_there, 0, c_there), device_id_type=MESH,
                ).start()

    def answer_first():
        take(0, 0)
        blank = [jnp.zeros((104, 128), F32)]
        halves = [[rb[pl.ds(2 * k + half, 8, stride=8), :] for k in range(CAP)] for half in range(2)]
        high, mid = split2(jnp.concatenate([jnp.concatenate(half + blank, axis=0) for half in halves], axis=1))
        qb[pl.ds(0, 8), 0, :] = by_source(values_of(items_of(0, 8), high, mid), 8)
        reply_to(0)

    def answer(p, first=True):
        if first:
            take(p, 0)
        take(p, 1)
        high, mid = arrived(p)
        info = items_of(256 * p, 32)
        values = values_of(info, high, mid)
        reply = by_source(values, 32)
        if first:
            qb[pl.ds(32 * p, 32), 0, :] = reply
            send(p, qb, ret, send2_sem, recv2_sem.at[z], lambda r: r)
        else:
            qb[pl.ds(8, 24), 0, :] = reply[8:32]
            for y_there in (1, 3, 2):
                reply_to(y_there)
        info_v[pl.ds(24 * p, 24), :] = jnp.concatenate([info[0:12]] + values + [jnp.zeros((8, 128), F32)], axis=0)

    for p in range(4):
        give(p)

    @pl.when(z < 2)
    def _():
        answer(0)

    @pl.when(z >= 2)
    def _():
        answer_first()
        answer(0, False)

    for p in range(1, 4):
        answer(p)

    sink = jnp.zeros((256, 256), F32)
    for p in range(4):
        info = info_v[pl.ds(24 * p, 24), :]
        drawn = info[4:8] + info[8:12] * info[12:16]
        spread = jnp.concatenate([jnp.broadcast_to(drawn[f : f + 1], (64, 128)) for f in range(4)], axis=0)
        share_high, share_mid = split2(jnp.where(tiles == info[0:1], spread, 0.0))
        high, mid = arrived(p)
        sink = sink + dot(share_high, high) + dot(share_high, mid) + dot(share_mid, high)
    for f in range(4):
        for half in range(2):
            sink_v[pl.ds(4 * half + f, 64, stride=8), :] = sink[64 * f : 64 * f + 64, 128 * half : 128 * half + 128]
    @pl.when(jnp.logical_not((z == 0) & (x < 2) & (y < 2)))
    def _():
        whole()


    for p in range(4):
        view = ret.at[pl.ds(0, 32)]
        pltpu.make_async_copy(view, view, recv2_sem.at[p]).wait()
    view = sb.at[pl.ds(0, 127 * MESSAGE), :]
    pltpu.make_async_copy(view, view, send_sem).wait()
    view = qb.at[pl.ds(0, 127)]
    pltpu.make_async_copy(view, view, send2_sem).wait()


def finish(pm, um, sel, sink, ret, next_o, sink_o, last, next_v, out_sems):
    sink_copy = pltpu.make_async_copy(sink, sink_o, out_sems.at[2])
    sink_copy.start()
    back = jnp.concatenate(split2(ret[:, 0, :].T[0:32]), axis=0)
    bound = jnp.zeros((8, 256), F32)
    for k in range(CAP):
        part = dot(back, sel[pl.ds(128 * k, 128), :])
        bound = bound + part[8 * k : 8 * k + 8] + part[32 + 8 * k : 40 + 8 * k]
    bound = jnp.concatenate([bound[0:4, :128], bound[0:4, 128:]], axis=0)
    for r in range(NR - 32, NR):
        last[row(r - NR + 32), :] = pm[row(r), :] + bound * um[row(r), :]
    for half in range(2):
        for f in range(4):
            j = 4 * half + f
            block = jnp.concatenate(
                [pm[pl.ds(j, NR - 32, stride=8), :], last[pl.ds(j, 32, stride=8), :]], axis=0
            )
            next_v[pl.ds(512 * half + f, 128, stride=4), :] = block.T
        rows = pl.ds(512 * half, 512)
        pltpu.make_async_copy(next_v.at[rows, :], next_o.at[rows, :], out_sems.at[half]).start()
    for half in range(2):
        rows = pl.ds(512 * half, 512)
        pltpu.make_async_copy(next_v.at[rows, :], next_o.at[rows, :], out_sems.at[half]).wait()
    sink_copy.wait()


def on_device(
    soil_field, rhizosphere, conductance, uptake_rate, segment_weight, segment_target, segment_tile, segment_count
):
    soil = soil_field.reshape(64, 4, 2, 128).transpose(0, 2, 1, 3).reshape(512, 128)
    vm, dma = pltpu.VMEM, pltpu.SemaphoreType.DMA
    any_spec, vmem_spec = pl.BlockSpec(memory_space=pl.ANY), pl.BlockSpec(memory_space=pltpu.VMEM)

    def hbm(a):
        return pltpu.with_memory_space_constraint(a, pltpu.HBM)

    pm, um, sel, sink, ret = pl.pallas_call(
        exchange,
        out_shape=(
            vm((1024, 128), F32), vm((1024, 128), F32), vm((384, 256), BF16), vm((512, 128), F32), vm((128, 1, 128), F32),
        ),
        in_specs=[any_spec] * 7 + [pl.BlockSpec(memory_space=pltpu.SMEM)],
        out_specs=(vmem_spec,) * 5,
        scratch_shapes=[
            vm((512, 128), F32), vm((1024, 128), F32), vm((1024, 128), F32), vm((4, 256), F32), vm((256, 256), F32),
            vm((1, 256), jnp.int32), vm((1, 256), jnp.int32), vm((1024, 128), F32), vm((1024, 128), F32),
            vm((1024, 128), F32), vm((1024, 128), F32), vm((128, 1, 128), F32), vm((96, 128), F32),
            dma((7,)), pltpu.SemaphoreType.REGULAR((4,)), dma(()), dma((8,)), dma(()), dma((4,)),
        ],
        compiler_params=pltpu.CompilerParams(
            collective_id=0, has_side_effects=True, vmem_limit_bytes=32 * 1024 * 1024
        ),
    )(
        hbm(soil),
        hbm(rhizosphere.reshape(1024, 128)),
        hbm(conductance.reshape(1024, 128)),
        hbm(uptake_rate.T),
        hbm(segment_weight),
        hbm(segment_target.reshape(1, 256)),
        hbm(segment_tile.reshape(1, 256)),
        segment_count,
    )
    nxt, sink = pl.pallas_call(
        finish,
        out_shape=(jax.ShapeDtypeStruct((1024, 128), F32), jax.ShapeDtypeStruct((512, 128), F32)),
        in_specs=[vmem_spec] * 5,
        out_specs=(any_spec,) * 2,
        scratch_shapes=[vm((256, 128), F32), vm((1024, 128), F32), dma((3,))],
        compiler_params=pltpu.CompilerParams(vmem_limit_bytes=16 * 1024 * 1024),
    )(*(pltpu.with_memory_space_constraint(a, pltpu.VMEM) for a in (pm, um, sel, sink, ret)))
    sink = sink.reshape(64, 2, 4, 128).transpose(0, 2, 1, 3)
    return nxt.reshape(256, 4, 128), sink.reshape(8, 8, 4, 256)


def solution(mesh):
    flat = ("gx", "gy")
    return jax.shard_map(
        on_device,
        mesh=mesh,
        in_specs=(
            P("gx", "gy", None, None), P(flat, None, None), P(flat, None, None), P(flat, None), P(flat, None),
            P(flat, None), P(flat), P(flat),
        ),
        out_specs=(P(flat, None, None), P("gx", "gy", None, None)),
        check_vma=False,
    )
```

```python
import itertools

import jax
import jax.numpy as jnp
from jax import lax
from jax.experimental import pallas as pl
from jax.experimental.pallas import tpu as pltpu
from jax.sharding import PartitionSpec as P

SUB = 32
CAP = 3
NR = 128
F32 = jnp.float32
BF16 = jnp.bfloat16
MESH = pl.DeviceIdType.MESH
NN = (((1,), (0,)), ((), ()))
NT = (((1,), (1,)), ((), ()))


MESSAGE = 7


def hops(o):
    return sum(min(v, 4 - v) for v in o[:2])


PLANE = sorted((o for o in itertools.product(range(4), range(4), range(2)) if any(o)), key=lambda o: (-hops(o), o))


def coords():
    gx, gy = lax.axis_index("gx"), lax.axis_index("gy")
    return gy // 2, gx // 4, lax.rem(gx, 4), lax.rem(gy, 2)


def device(x, y, z, c):
    return y * 4 + z, x * 2 + c


def place(x, y, z, c):
    return z * 32 + y * 8 + x * 2 + c


def dot(a, b, dims=NN):
    return lax.dot_general(a, b, dims, preferred_element_type=F32)


def split2(x):
    high = x.astype(BF16)
    return high, (x - high.astype(F32)).astype(BF16)


def split3(x):
    high, mid = split2(x)
    return high, mid, (x - high.astype(F32) - mid.astype(F32)).astype(BF16)


def row(r):
    return pl.ds(8 * r, 8)


def double_step(level, cond, low, boundary, uptake):
    l0 = level[row(low), :]
    zero = jnp.zeros((8, 128), F32)
    p0 = uptake * l0 if uptake is not None else zero
    p1 = l1 = cp = None
    for r in range(low, NR):
        c = cond[row(r), :]
        outer = level[row(r + 1), :] if r < NR - 1 else boundary
        cur = c * (outer - l0)
        new = l0 + cur - p0 if p0 is not None else l0 + cur
        p0, l0 = cur, outer
        if r == low:
            p1 = uptake * new if uptake is not None else zero
        else:
            cur1 = cp * (new - l1)
            level[row(r - 1), :] = l1 + cur1 - p1
            p1 = cur1
        l1, cp = new, c
    cur1 = cp * (boundary - l1)
    level[row(NR - 1), :] = l1 + cur1 - p1
    return p0 + cur1


def exchange(
    soil_h, rhiz_h, cond_h, upt_h, w_h, tgt_h, tile_h, cnt_s,
    pm, um, sel, sink_v, ret,
    soil_v, rhiz_v, cond_v, upt_v, w_v, tgt_v, tile_v,
    cm, tm, sb, rb, qb, info_v,
    in_sems, plane_sem, send_sem, recv_sem, send2_sem, recv2_sem,
):
    x, y, z, c = coords()
    me = place(x, y, z, c)
    loads = [
        pltpu.make_async_copy(s, d, in_sems.at[i])
        for i, (s, d) in enumerate(
            [(tgt_h, tgt_v), (tile_h, tile_v), (w_h, w_v), (cond_h, cond_v), (rhiz_h, rhiz_v), (upt_h, upt_v), (soil_h, soil_v)]
        )
    ]

    def beside(o):
        return (x + o[0]) & 3, (y + o[1]) & 3, c ^ o[2]

    barrier = pltpu.get_barrier_semaphore()
    for o in PLANE:
        ox, oy, oc = beside(o)
        pl.semaphore_signal(barrier, inc=1, device_id=device(ox, oy, z, oc), device_id_type=MESH)
    for load in loads:
        load.start()
    count = cnt_s[0]

    def send(p, src, dst, send_s, recv_s, rows):
        def copy_to(x, y, c):
            there = place(x, y, p, c)
            return pltpu.make_async_remote_copy(
                src.at[rows(there)], dst.at[rows(me)], send_s, recv_s,
                device_id=device(x, y, p, c), device_id_type=MESH,
            )

        for o in PLANE:
            copy_to(*beside(o)).start()

        @pl.when(z != p)
        def _():
            copy_to(x, y, c).start()

        @pl.when(z == p)
        def _():
            pltpu.make_async_copy(src.at[rows(me)], dst.at[rows(me)], recv_s).start()

    def block(r):
        return pl.ds(8 * r, MESSAGE)

    for load in loads[:3]:
        load.wait()
    live = lax.broadcasted_iota(jnp.int32, (1, 256), 1) < count
    names = lax.broadcasted_iota(jnp.int32, (128, 256), 0)
    target = tgt_v[...]
    target = ((target >> 3) & 3) * 32 + (target >> 5) * 8 + (target & 7)
    match = jnp.where((names == target) & live, 1.0, 0.0)
    before = jnp.where(
        lax.broadcasted_iota(jnp.int32, (256, 256), 0) < lax.broadcasted_iota(jnp.int32, (256, 256), 1), 1.0, 0.0
    ).astype(BF16)
    rank = dot(match.astype(BF16), before)
    for k in range(CAP):
        sel[pl.ds(128 * k, 128), :] = jnp.where(rank == k, match, 0.0).astype(BF16)
    w = w_v[...]
    portion = w / jnp.sum(w, axis=1, keepdims=True)
    high, mid = split2(portion)
    for k in range(CAP):
        pick = sel[pl.ds(128 * k, 128), :]
        rows = dot(pick, high) + dot(pick, mid)
        sb[pl.ds(2 * k, 128, stride=8), :] = rows[:, :128]
        sb[pl.ds(2 * k + 1, 128, stride=8), :] = rows[:, 128:]

    for load in loads[3:6]:
        load.wait()
    lives = [lax.broadcasted_iota(jnp.int32, (1, 128), 1) + 128 * half < count for half in range(2)]
    for j in range(8):
        half, f = j // 4, j % 4
        rows = pl.ds(512 * half + f, 128, stride=4)
        pm[pl.ds(j, 128, stride=8), :] = rhiz_v[rows, :].T
        cm[pl.ds(j, 128, stride=8), :] = jnp.where(lives[half], cond_v[rows, :].T, 0.0)
    uptake = jnp.concatenate(
        [jnp.where(lives[half], upt_v[:, pl.ds(128 * half, 128)], 0.0) for half in range(2)], axis=0
    )

    def tell():
        pl.semaphore_wait(barrier, len(PLANE) + z)
        for dz in (1, 2, 3):

            @pl.when(z >= dz)
            def _():
                pl.semaphore_signal(plane_sem.at[z], inc=1, device_id=device(x, y, z - dz, c), device_id_type=MESH)

            @pl.when(z + dz < 4)
            def _():
                pl.semaphore_signal(barrier, inc=1, device_id=device(x, y, z + dz, c), device_id_type=MESH)

    late = (x >= 1) & (y >= 1)
    pl.when(late)(tell)

    zero, one = jnp.zeros((8, 128), F32), jnp.ones((8, 128), F32)
    for r in range(NR - 32, NR):
        tm[row(r), :] = pm[row(r), :]
        um[row(r), :] = zero
    drawn0, gain = zero, zero
    for g in range(4):
        drawn0 = lax.fori_loop(0, 4, lambda i, d, g=g: d + double_step(tm, cm, NR - 32 + 8 * g, zero, None), drawn0)
        gain = lax.fori_loop(0, 4, lambda i, d, g=g: d + double_step(um, cm, NR - 8 - 8 * g, one, None), gain)

    def as_rows(v):
        return jnp.concatenate([v[0:4], v[4:8]], axis=1)

    tile_row = tile_v[...].astype(F32)
    items = jnp.concatenate(
        [tile_row, jnp.zeros((3, 256), F32), as_rows(drawn0), as_rows(gain), jnp.zeros((4, 256), F32)], axis=0
    )
    meta = jnp.zeros((128, 128), F32)
    for k in range(CAP):
        parts = [jnp.zeros((32 * k, 256), F32)] if k else []
        wide = jnp.concatenate(parts + [items, jnp.zeros((112 - 32 * k, 256), F32)], axis=0)
        pick = sel[pl.ds(128 * k, 128), :]
        for piece in split3(wide):
            meta = meta + dot(pick, piece, NT)
    sb[pl.ds(6, 128, stride=8), :] = meta


    def arrived(p):
        blank = [jnp.zeros((32, 128), F32)]
        halves = [[rb[pl.ds(256 * p + 2 * k + half, 32, stride=8), :] for k in range(CAP)] for half in range(2)]
        return split2(jnp.concatenate([jnp.concatenate(half + blank, axis=0) for half in halves], axis=1))

    def whole():
        lax.fori_loop(0, SUB // 2, lambda i, d: d + double_step(pm, cm, 0, zero, uptake), zero)

    @pl.when((z == 0) & (x < 2) & (y < 2))
    def _():
        whole()

    pl.when(jnp.logical_not(late))(tell)

    def give(p):
        @pl.when(z < p)
        def _():
            pl.semaphore_wait(plane_sem.at[p], 1)

        send(p, sb, rb, send_sem, recv_sem.at[2 * z + jnp.minimum(y, 1)], block)

    def take(p, part):
        view = rb.at[pl.ds(0, (8, 24)[part] * MESSAGE), :]
        pltpu.make_async_copy(view, view, recv_sem.at[2 * p + part]).wait()

    def values_of(info, high, mid):
        field = dot(soil_high, high, NT) + dot(soil_high, mid, NT) + dot(soil_mid, high, NT)
        masked = jnp.where(tiles == info[0:1], field, 0.0)
        return [jnp.sum(masked[64 * f : 64 * f + 64], axis=0, keepdims=True) for f in range(4)]

    def items_of(start, n):
        items = rb[pl.ds(start + 6, n, stride=8), :]
        rest = jnp.full((128 - 3 * n, 128), -1.0, F32)
        return jnp.concatenate([items, pltpu.roll(items, 96, 1), pltpu.roll(items, 64, 1), rest], axis=0).T

    def by_source(values, n):
        reply = jnp.concatenate(values + [jnp.zeros((124, 128), F32)], axis=0).T
        return reply[0:n] + pltpu.roll(reply[n : 2 * n], 8, 1) + pltpu.roll(reply[2 * n : 3 * n], 16, 1)

    def reply_to(y_there):
        for x_there in (0, 1, 3, 2):
            for c_there in range(2):
                there = place(x_there, y_there, 0, c_there)
                pltpu.make_async_remote_copy(
                    qb.at[there], ret.at[me], send2_sem, recv2_sem.at[z],
                    device_id=device(x_there, y_there, 0, c_there), device_id_type=MESH,
                ).start()

    def answer_first():
        take(0, 0)
        blank = [jnp.zeros((104, 128), F32)]
        halves = [[rb[pl.ds(2 * k + half, 8, stride=8), :] for k in range(CAP)] for half in range(2)]
        high, mid = split2(jnp.concatenate([jnp.concatenate(half + blank, axis=0) for half in halves], axis=1))
        qb[pl.ds(0, 8), 0, :] = by_source(values_of(items_of(0, 8), high, mid), 8)
        reply_to(0)

    def answer(p, first=True):
        if first:
            take(p, 0)
        take(p, 1)
        high, mid = arrived(p)
        info = items_of(256 * p, 32)
        values = values_of(info, high, mid)
        reply = by_source(values, 32)
        if first:
            qb[pl.ds(32 * p, 32), 0, :] = reply
            send(p, qb, ret, send2_sem, recv2_sem.at[z], lambda r: r)
        else:
            qb[pl.ds(8, 24), 0, :] = reply[8:32]
            for y_there in (1, 3, 2):
                reply_to(y_there)
        info_v[pl.ds(24 * p, 24), :] = jnp.concatenate([info[0:12]] + values + [jnp.zeros((8, 128), F32)], axis=0)

    for p in range(4):
        give(p)

    loads[6].wait()
    soil = jnp.concatenate(
        [
            jnp.concatenate([soil_v[pl.ds(4 * half + f, 64, stride=8), :] for half in range(2)], axis=1)
            for f in range(4)
        ],
        axis=0,
    )
    soil_high, soil_mid = split2(soil)
    tiles = (lax.broadcasted_iota(jnp.int32, (256, 128), 0) & 63).astype(F32)

    @pl.when(z < 2)
    def _():
        answer(0)

    @pl.when(z >= 2)
    def _():
        answer_first()
        answer(0, False)

    for p in range(1, 4):
        answer(p)

    sink = jnp.zeros((256, 256), F32)
    for p in range(4):
        info = info_v[pl.ds(24 * p, 24), :]
        drawn = info[4:8] + info[8:12] * info[12:16]
        spread = jnp.concatenate([jnp.broadcast_to(drawn[f : f + 1], (64, 128)) for f in range(4)], axis=0)
        share_high, share_mid = split2(jnp.where(tiles == info[0:1], spread, 0.0))
        high, mid = arrived(p)
        sink = sink + dot(share_high, high) + dot(share_high, mid) + dot(share_mid, high)
    for f in range(4):
        for half in range(2):
            sink_v[pl.ds(4 * half + f, 64, stride=8), :] = sink[64 * f : 64 * f + 64, 128 * half : 128 * half + 128]
    @pl.when(jnp.logical_not((z == 0) & (x < 2) & (y < 2)))
    def _():
        whole()


    for p in range(4):
        view = ret.at[pl.ds(0, 32)]
        pltpu.make_async_copy(view, view, recv2_sem.at[p]).wait()
    view = sb.at[pl.ds(0, 127 * MESSAGE), :]
    pltpu.make_async_copy(view, view, send_sem).wait()
    view = qb.at[pl.ds(0, 127)]
    pltpu.make_async_copy(view, view, send2_sem).wait()


def finish(pm, um, sel, sink, ret, next_o, sink_o, last, next_v, out_sems):
    sink_copy = pltpu.make_async_copy(sink, sink_o, out_sems.at[2])
    sink_copy.start()
    back = jnp.concatenate(split2(ret[:, 0, :].T[0:32]), axis=0)
    bound = jnp.zeros((8, 256), F32)
    for k in range(CAP):
        part = dot(back, sel[pl.ds(128 * k, 128), :])
        bound = bound + part[8 * k : 8 * k + 8] + part[32 + 8 * k : 40 + 8 * k]
    bound = jnp.concatenate([bound[0:4, :128], bound[0:4, 128:]], axis=0)
    for r in range(NR - 32, NR):
        last[row(r - NR + 32), :] = pm[row(r), :] + bound * um[row(r), :]
    for half in range(2):
        for f in range(4):
            j = 4 * half + f
            block = jnp.concatenate(
                [pm[pl.ds(j, NR - 32, stride=8), :], last[pl.ds(j, 32, stride=8), :]], axis=0
            )
            next_v[pl.ds(512 * half + f, 128, stride=4), :] = block.T
        rows = pl.ds(512 * half, 512)
        pltpu.make_async_copy(next_v.at[rows, :], next_o.at[rows, :], out_sems.at[half]).start()
    for half in range(2):
        rows = pl.ds(512 * half, 512)
        pltpu.make_async_copy(next_v.at[rows, :], next_o.at[rows, :], out_sems.at[half]).wait()
    sink_copy.wait()


def on_device(
    soil_field, rhizosphere, conductance, uptake_rate, segment_weight, segment_target, segment_tile, segment_count
):
    soil = soil_field.reshape(64, 4, 2, 128).transpose(0, 2, 1, 3).reshape(512, 128)
    vm, dma = pltpu.VMEM, pltpu.SemaphoreType.DMA
    any_spec, vmem_spec = pl.BlockSpec(memory_space=pl.ANY), pl.BlockSpec(memory_space=pltpu.VMEM)

    def hbm(a):
        return pltpu.with_memory_space_constraint(a, pltpu.HBM)

    pm, um, sel, sink, ret = pl.pallas_call(
        exchange,
        out_shape=(
            vm((1024, 128), F32), vm((1024, 128), F32), vm((384, 256), BF16), vm((512, 128), F32), vm((128, 1, 128), F32),
        ),
        in_specs=[any_spec] * 7 + [pl.BlockSpec(memory_space=pltpu.SMEM)],
        out_specs=(vmem_spec,) * 5,
        scratch_shapes=[
            vm((512, 128), F32), vm((1024, 128), F32), vm((1024, 128), F32), vm((4, 256), F32), vm((256, 256), F32),
            vm((1, 256), jnp.int32), vm((1, 256), jnp.int32), vm((1024, 128), F32), vm((1024, 128), F32),
            vm((1024, 128), F32), vm((1024, 128), F32), vm((128, 1, 128), F32), vm((96, 128), F32),
            dma((7,)), pltpu.SemaphoreType.REGULAR((4,)), dma(()), dma((8,)), dma(()), dma((4,)),
        ],
        compiler_params=pltpu.CompilerParams(
            collective_id=0, has_side_effects=True, vmem_limit_bytes=32 * 1024 * 1024
        ),
    )(
        hbm(soil),
        hbm(rhizosphere.reshape(1024, 128)),
        hbm(conductance.reshape(1024, 128)),
        hbm(uptake_rate.T),
        hbm(segment_weight),
        hbm(segment_target.reshape(1, 256)),
        hbm(segment_tile.reshape(1, 256)),
        segment_count,
    )
    nxt, sink = pl.pallas_call(
        finish,
        out_shape=(jax.ShapeDtypeStruct((1024, 128), F32), jax.ShapeDtypeStruct((512, 128), F32)),
        in_specs=[vmem_spec] * 5,
        out_specs=(any_spec,) * 2,
        scratch_shapes=[vm((256, 128), F32), vm((1024, 128), F32), dma((3,))],
        compiler_params=pltpu.CompilerParams(vmem_limit_bytes=16 * 1024 * 1024),
    )(*(pltpu.with_memory_space_constraint(a, pltpu.VMEM) for a in (pm, um, sel, sink, ret)))
    sink = sink.reshape(64, 2, 4, 128).transpose(0, 2, 1, 3)
    return nxt.reshape(256, 4, 128), sink.reshape(8, 8, 4, 256)


def solution(mesh):
    flat = ("gx", "gy")
    return jax.shard_map(
        on_device,
        mesh=mesh,
        in_specs=(
            P("gx", "gy", None, None), P(flat, None, None), P(flat, None, None), P(flat, None), P(flat, None),
            P(flat, None), P(flat), P(flat),
        ),
        out_specs=(P(flat, None, None), P("gx", "gy", None, None)),
        check_vma=False,
    )
```

```python
import itertools

import jax
import jax.numpy as jnp
from jax import lax
from jax.experimental import pallas as pl
from jax.experimental.pallas import tpu as pltpu
from jax.sharding import PartitionSpec as P

SUB = 32
CAP = 3
NR = 128
F32 = jnp.float32
BF16 = jnp.bfloat16
MESH = pl.DeviceIdType.MESH
NN = (((1,), (0,)), ((), ()))
NT = (((1,), (1,)), ((), ()))


MESSAGE = 7


def hops(o):
    return sum(min(v, 4 - v) for v in o[:2])


PLANE = sorted((o for o in itertools.product(range(4), range(4), range(2)) if any(o)), key=lambda o: (-hops(o), o))


def coords():
    gx, gy = lax.axis_index("gx"), lax.axis_index("gy")
    return gy // 2, gx // 4, lax.rem(gx, 4), lax.rem(gy, 2)


def device(x, y, z, c):
    return y * 4 + z, x * 2 + c


def place(x, y, z, c):
    return z * 32 + y * 8 + x * 2 + c


def dot(a, b, dims=NN):
    return lax.dot_general(a, b, dims, preferred_element_type=F32)


def split2(x):
    high = x.astype(BF16)
    return high, (x - high.astype(F32)).astype(BF16)


def split3(x):
    high, mid = split2(x)
    return high, mid, (x - high.astype(F32) - mid.astype(F32)).astype(BF16)


def row(r):
    return pl.ds(8 * r, 8)


def double_step(level, cond, low, boundary, uptake):
    l0 = level[row(low), :]
    zero = jnp.zeros((8, 128), F32)
    p0 = uptake * l0 if uptake is not None else zero
    p1 = l1 = cp = None
    for r in range(low, NR):
        c = cond[row(r), :]
        outer = level[row(r + 1), :] if r < NR - 1 else boundary
        cur = c * (outer - l0)
        new = l0 + cur - p0 if p0 is not None else l0 + cur
        p0, l0 = cur, outer
        if r == low:
            p1 = uptake * new if uptake is not None else zero
        else:
            cur1 = cp * (new - l1)
            level[row(r - 1), :] = l1 + cur1 - p1
            p1 = cur1
        l1, cp = new, c
    cur1 = cp * (boundary - l1)
    level[row(NR - 1), :] = l1 + cur1 - p1
    return p0 + cur1


def exchange(
    soil_h, rhiz_h, cond_h, upt_h, w_h, tgt_h, tile_h, cnt_s,
    pm, um, sel, sink_v, ret,
    soil_v, rhiz_v, cond_v, upt_v, w_v, tgt_v, tile_v,
    cm, tm, sb, rb, qb, info_v,
    in_sems, plane_sem, send_sem, recv_sem, send2_sem, recv2_sem,
):
    x, y, z, c = coords()
    me = place(x, y, z, c)
    loads = [
        pltpu.make_async_copy(s, d, in_sems.at[i])
        for i, (s, d) in enumerate(
            [(tgt_h, tgt_v), (tile_h, tile_v), (w_h, w_v), (cond_h, cond_v), (rhiz_h, rhiz_v), (upt_h, upt_v), (soil_h, soil_v)]
        )
    ]

    def beside(o):
        return (x + o[0]) & 3, (y + o[1]) & 3, c ^ o[2]

    barrier = pltpu.get_barrier_semaphore()
    for o in PLANE:
        ox, oy, oc = beside(o)
        pl.semaphore_signal(barrier, inc=1, device_id=device(ox, oy, z, oc), device_id_type=MESH)
    for load in loads:
        load.start()
    count = cnt_s[0]

    def send(p, src, dst, send_s, recv_s, rows):
        def copy_to(x, y, c):
            there = place(x, y, p, c)
            return pltpu.make_async_remote_copy(
                src.at[rows(there)], dst.at[rows(me)], send_s, recv_s,
                device_id=device(x, y, p, c), device_id_type=MESH,
            )

        for o in PLANE:
            copy_to(*beside(o)).start()

        @pl.when(z != p)
        def _():
            copy_to(x, y, c).start()

        @pl.when(z == p)
        def _():
            pltpu.make_async_copy(src.at[rows(me)], dst.at[rows(me)], recv_s).start()

    def block(r):
        return pl.ds(8 * r, MESSAGE)

    for load in loads[:3]:
        load.wait()
    live = lax.broadcasted_iota(jnp.int32, (1, 256), 1) < count
    names = lax.broadcasted_iota(jnp.int32, (128, 256), 0)
    target = tgt_v[...]
    target = ((target >> 3) & 3) * 32 + (target >> 5) * 8 + (target & 7)
    match = jnp.where((names == target) & live, 1.0, 0.0)
    before = jnp.where(
        lax.broadcasted_iota(jnp.int32, (256, 256), 0) < lax.broadcasted_iota(jnp.int32, (256, 256), 1), 1.0, 0.0
    ).astype(BF16)
    rank = dot(match.astype(BF16), before)
    for k in range(CAP):
        sel[pl.ds(128 * k, 128), :] = jnp.where(rank == k, match, 0.0).astype(BF16)
    w = w_v[...]
    portion = w / jnp.sum(w, axis=1, keepdims=True)
    high, mid = split2(portion)
    for k in range(CAP):
        pick = sel[pl.ds(128 * k, 128), :]
        rows = dot(pick, high) + dot(pick, mid)
        sb[pl.ds(2 * k, 128, stride=8), :] = rows[:, :128]
        sb[pl.ds(2 * k + 1, 128, stride=8), :] = rows[:, 128:]

    for load in loads[3:6]:
        load.wait()
    lives = [lax.broadcasted_iota(jnp.int32, (1, 128), 1) + 128 * half < count for half in range(2)]
    for j in range(8):
        half, f = j // 4, j % 4
        rows = pl.ds(512 * half + f, 128, stride=4)
        pm[pl.ds(j, 128, stride=8), :] = rhiz_v[rows, :].T
        cm[pl.ds(j, 128, stride=8), :] = jnp.where(lives[half], cond_v[rows, :].T, 0.0)
    uptake = jnp.concatenate(
        [jnp.where(lives[half], upt_v[:, pl.ds(128 * half, 128)], 0.0) for half in range(2)], axis=0
    )

    def tell():
        pl.semaphore_wait(barrier, len(PLANE) + z)
        for dz in (3, 2, 1):

            @pl.when(z >= dz)
            def _():
                pl.semaphore_signal(plane_sem.at[z], inc=1, device_id=device(x, y, z - dz, c), device_id_type=MESH)

        for dz in (1, 2, 3):

            @pl.when(z + dz < 4)
            def _():
                pl.semaphore_signal(barrier, inc=1, device_id=device(x, y, z + dz, c), device_id_type=MESH)

    late = (x >= 1) & (y >= 1)
    pl.when(late)(tell)

    zero, one = jnp.zeros((8, 128), F32), jnp.ones((8, 128), F32)
    for r in range(NR - 32, NR):
        tm[row(r), :] = pm[row(r), :]
        um[row(r), :] = zero
    drawn0, gain = zero, zero
    for g in range(4):
        drawn0 = lax.fori_loop(0, 4, lambda i, d, g=g: d + double_step(tm, cm, NR - 32 + 8 * g, zero, None), drawn0)
        gain = lax.fori_loop(0, 4, lambda i, d, g=g: d + double_step(um, cm, NR - 8 - 8 * g, one, None), gain)

    def as_rows(v):
        return jnp.concatenate([v[0:4], v[4:8]], axis=1)

    tile_row = tile_v[...].astype(F32)
    items = jnp.concatenate(
        [tile_row, jnp.zeros((3, 256), F32), as_rows(drawn0), as_rows(gain), jnp.zeros((4, 256), F32)], axis=0
    )
    meta = jnp.zeros((128, 128), F32)
    for k in range(CAP):
        parts = [jnp.zeros((32 * k, 256), F32)] if k else []
        wide = jnp.concatenate(parts + [items, jnp.zeros((112 - 32 * k, 256), F32)], axis=0)
        pick = sel[pl.ds(128 * k, 128), :]
        for piece in split3(wide):
            meta = meta + dot(pick, piece, NT)
    sb[pl.ds(6, 128, stride=8), :] = meta


    def arrived(p):
        blank = [jnp.zeros((32, 128), F32)]
        halves = [[rb[pl.ds(256 * p + 2 * k + half, 32, stride=8), :] for k in range(CAP)] for half in range(2)]
        return split2(jnp.concatenate([jnp.concatenate(half + blank, axis=0) for half in halves], axis=1))

    def whole():
        lax.fori_loop(0, SUB // 2, lambda i, d: d + double_step(pm, cm, 0, zero, uptake), zero)

    @pl.when((z == 0) & (x < 2) & (y < 2))
    def _():
        whole()

    pl.when(jnp.logical_not(late))(tell)

    def give(p):
        @pl.when(z < p)
        def _():
            pl.semaphore_wait(plane_sem.at[p], 1)

        send(p, sb, rb, send_sem, recv_sem.at[2 * z + jnp.minimum(y, 1)], block)

    def take(p, part):
        view = rb.at[pl.ds(0, (8, 24)[part] * MESSAGE), :]
        pltpu.make_async_copy(view, view, recv_sem.at[2 * p + part]).wait()

    def values_of(info, high, mid):
        field = dot(soil_high, high, NT) + dot(soil_high, mid, NT) + dot(soil_mid, high, NT)
        masked = jnp.where(tiles == info[0:1], field, 0.0)
        return [jnp.sum(masked[64 * f : 64 * f + 64], axis=0, keepdims=True) for f in range(4)]

    def items_of(start, n):
        items = rb[pl.ds(start + 6, n, stride=8), :]
        rest = jnp.full((128 - 3 * n, 128), -1.0, F32)
        return jnp.concatenate([items, pltpu.roll(items, 96, 1), pltpu.roll(items, 64, 1), rest], axis=0).T

    def by_source(values, n):
        reply = jnp.concatenate(values + [jnp.zeros((124, 128), F32)], axis=0).T
        return reply[0:n] + pltpu.roll(reply[n : 2 * n], 8, 1) + pltpu.roll(reply[2 * n : 3 * n], 16, 1)

    def reply_to(y_there):
        for x_there in (0, 1, 3, 2):
            for c_there in range(2):
                there = place(x_there, y_there, 0, c_there)
                pltpu.make_async_remote_copy(
                    qb.at[there], ret.at[me], send2_sem, recv2_sem.at[z],
                    device_id=device(x_there, y_there, 0, c_there), device_id_type=MESH,
                ).start()

    def answer_first():
        take(0, 0)
        blank = [jnp.zeros((104, 128), F32)]
        halves = [[rb[pl.ds(2 * k + half, 8, stride=8), :] for k in range(CAP)] for half in range(2)]
        high, mid = split2(jnp.concatenate([jnp.concatenate(half + blank, axis=0) for half in halves], axis=1))
        qb[pl.ds(0, 8), 0, :] = by_source(values_of(items_of(0, 8), high, mid), 8)
        reply_to(0)

    def answer(p, first=True):
        if first:
            take(p, 0)
        take(p, 1)
        high, mid = arrived(p)
        info = items_of(256 * p, 32)
        values = values_of(info, high, mid)
        reply = by_source(values, 32)
        if first:
            qb[pl.ds(32 * p, 32), 0, :] = reply
            send(p, qb, ret, send2_sem, recv2_sem.at[z], lambda r: r)
        else:
            qb[pl.ds(8, 24), 0, :] = reply[8:32]
            for y_there in (1, 3, 2):
                reply_to(y_there)
        info_v[pl.ds(24 * p, 24), :] = jnp.concatenate([info[0:12]] + values + [jnp.zeros((8, 128), F32)], axis=0)

    for p in range(4):
        give(p)

    loads[6].wait()
    soil = jnp.concatenate(
        [
            jnp.concatenate([soil_v[pl.ds(4 * half + f, 64, stride=8), :] for half in range(2)], axis=1)
            for f in range(4)
        ],
        axis=0,
    )
    soil_high, soil_mid = split2(soil)
    tiles = (lax.broadcasted_iota(jnp.int32, (256, 128), 0) & 63).astype(F32)

    @pl.when(z < 2)
    def _():
        answer(0)

    @pl.when(z >= 2)
    def _():
        answer_first()
        answer(0, False)

    for p in range(1, 4):
        answer(p)

    sink = jnp.zeros((256, 256), F32)
    for p in range(4):
        info = info_v[pl.ds(24 * p, 24), :]
        drawn = info[4:8] + info[8:12] * info[12:16]
        spread = jnp.concatenate([jnp.broadcast_to(drawn[f : f + 1], (64, 128)) for f in range(4)], axis=0)
        share_high, share_mid = split2(jnp.where(tiles == info[0:1], spread, 0.0))
        high, mid = arrived(p)
        sink = sink + dot(share_high, high) + dot(share_high, mid) + dot(share_mid, high)
    for f in range(4):
        for half in range(2):
            sink_v[pl.ds(4 * half + f, 64, stride=8), :] = sink[64 * f : 64 * f + 64, 128 * half : 128 * half + 128]
    @pl.when(jnp.logical_not((z == 0) & (x < 2) & (y < 2)))
    def _():
        whole()


    for p in range(4):
        view = ret.at[pl.ds(0, 32)]
        pltpu.make_async_copy(view, view, recv2_sem.at[p]).wait()
    view = sb.at[pl.ds(0, 127 * MESSAGE), :]
    pltpu.make_async_copy(view, view, send_sem).wait()
    view = qb.at[pl.ds(0, 127)]
    pltpu.make_async_copy(view, view, send2_sem).wait()


def finish(pm, um, sel, sink, ret, next_o, sink_o, last, next_v, out_sems):
    sink_copy = pltpu.make_async_copy(sink, sink_o, out_sems.at[2])
    sink_copy.start()
    back = jnp.concatenate(split2(ret[:, 0, :].T[0:32]), axis=0)
    bound = jnp.zeros((8, 256), F32)
    for k in range(CAP):
        part = dot(back, sel[pl.ds(128 * k, 128), :])
        bound = bound + part[8 * k : 8 * k + 8] + part[32 + 8 * k : 40 + 8 * k]
    bound = jnp.concatenate([bound[0:4, :128], bound[0:4, 128:]], axis=0)
    for r in range(NR - 32, NR):
        last[row(r - NR + 32), :] = pm[row(r), :] + bound * um[row(r), :]
    for half in range(2):
        for f in range(4):
            j = 4 * half + f
            block = jnp.concatenate(
                [pm[pl.ds(j, NR - 32, stride=8), :], last[pl.ds(j, 32, stride=8), :]], axis=0
            )
            next_v[pl.ds(512 * half + f, 128, stride=4), :] = block.T
        rows = pl.ds(512 * half, 512)
        pltpu.make_async_copy(next_v.at[rows, :], next_o.at[rows, :], out_sems.at[half]).start()
    for half in range(2):
        rows = pl.ds(512 * half, 512)
        pltpu.make_async_copy(next_v.at[rows, :], next_o.at[rows, :], out_sems.at[half]).wait()
    sink_copy.wait()


def on_device(
    soil_field, rhizosphere, conductance, uptake_rate, segment_weight, segment_target, segment_tile, segment_count
):
    soil = soil_field.reshape(64, 4, 2, 128).transpose(0, 2, 1, 3).reshape(512, 128)
    vm, dma = pltpu.VMEM, pltpu.SemaphoreType.DMA
    any_spec, vmem_spec = pl.BlockSpec(memory_space=pl.ANY), pl.BlockSpec(memory_space=pltpu.VMEM)

    def hbm(a):
        return pltpu.with_memory_space_constraint(a, pltpu.HBM)

    pm, um, sel, sink, ret = pl.pallas_call(
        exchange,
        out_shape=(
            vm((1024, 128), F32), vm((1024, 128), F32), vm((384, 256), BF16), vm((512, 128), F32), vm((128, 1, 128), F32),
        ),
        in_specs=[any_spec] * 7 + [pl.BlockSpec(memory_space=pltpu.SMEM)],
        out_specs=(vmem_spec,) * 5,
        scratch_shapes=[
            vm((512, 128), F32), vm((1024, 128), F32), vm((1024, 128), F32), vm((4, 256), F32), vm((256, 256), F32),
            vm((1, 256), jnp.int32), vm((1, 256), jnp.int32), vm((1024, 128), F32), vm((1024, 128), F32),
            vm((1024, 128), F32), vm((1024, 128), F32), vm((128, 1, 128), F32), vm((96, 128), F32),
            dma((7,)), pltpu.SemaphoreType.REGULAR((4,)), dma(()), dma((8,)), dma(()), dma((4,)),
        ],
        compiler_params=pltpu.CompilerParams(
            collective_id=0, has_side_effects=True, vmem_limit_bytes=32 * 1024 * 1024
        ),
    )(
        hbm(soil),
        hbm(rhizosphere.reshape(1024, 128)),
        hbm(conductance.reshape(1024, 128)),
        hbm(uptake_rate.T),
        hbm(segment_weight),
        hbm(segment_target.reshape(1, 256)),
        hbm(segment_tile.reshape(1, 256)),
        segment_count,
    )
    nxt, sink = pl.pallas_call(
        finish,
        out_shape=(jax.ShapeDtypeStruct((1024, 128), F32), jax.ShapeDtypeStruct((512, 128), F32)),
        in_specs=[vmem_spec] * 5,
        out_specs=(any_spec,) * 2,
        scratch_shapes=[vm((256, 128), F32), vm((1024, 128), F32), dma((3,))],
        compiler_params=pltpu.CompilerParams(vmem_limit_bytes=16 * 1024 * 1024),
    )(*(pltpu.with_memory_space_constraint(a, pltpu.VMEM) for a in (pm, um, sel, sink, ret)))
    sink = sink.reshape(64, 2, 4, 128).transpose(0, 2, 1, 3)
    return nxt.reshape(256, 4, 128), sink.reshape(8, 8, 4, 256)


def solution(mesh):
    flat = ("gx", "gy")
    return jax.shard_map(
        on_device,
        mesh=mesh,
        in_specs=(
            P("gx", "gy", None, None), P(flat, None, None), P(flat, None, None), P(flat, None), P(flat, None),
            P(flat, None), P(flat), P(flat),
        ),
        out_specs=(P(flat, None, None), P("gx", "gy", None, None)),
        check_vma=False,
    )
```
